128 devices in a mesh: head: 8 (over x, core), inner: 8 (over z, y_lo), outer: 2 (over y_hi).
Axes of the slice: x: 4, y: 4 (y_hi: 2, y_lo: 2; y = y_hi * 2 + y_lo), z: 4, core: 2. Of those that a mesh axis runs over, the one named last changes fastest.
Arguments:
- queries: bfloat16 [4096, 64, 128], P(('head', 'inner', 'outer')), may hold values from -162 to 162
- keys: bfloat16 [4096, 8, 128], P(('head', 'inner', 'outer')), may hold values from -6 to 6
- values: bfloat16 [4096, 8, 128], P(('head', 'inner', 'outer')), may hold values from -6 to 6
- out_states: bfloat16 [4096, 64, 128], P(('head', 'inner', 'outer')), may hold values from -6 to 6
- out_grads: bfloat16 [4096, 64, 128], P(('head', 'inner', 'outer')), may hold values from -6 to 6
- segment_ids: int32 [4096], replicated, may hold values from 0 to 7, never falling along the last dimension, each value on 1 to 2048 neighbouring positions
- span_position: int32 [128], replicated, may hold values from 0 to 127, each once
Outputs:
- query_grad: bfloat16 [4096, 64, 128], P(('head', 'inner', 'outer'))
- key_grad: bfloat16 [4096, 8, 128], P(('head', 'inner', 'outer'))
- value_grad: bfloat16 [4096, 8, 128], P(('head', 'inner', 'outer'))
The draws below stay inside these ranges and needn't reach their ends.
All inputs are finite; a program needn't handle non-finite values.
Results may differ from the reference program's by a relative error of at most 0.005.
Values may be sent and summed in bfloat16 or wider, within the bound.
No kernel may reach another device: no remote copies, remote signals or barrier semaphores. Data moves between devices by JAX's collectives and lax.ppermute only.
A program may use at most 64 MiB of HBM per device.

```python
import math
import jax
import jax.numpy as jnp
import numpy as np
from jax import lax

QUERY_HEADS = 64
KEY_VALUE_HEADS = 8
HEAD_SIZE = 128
TOK_DEV = 32
PACKED_TOKENS = 4096
SPANS = 128
SEGS = 8


def drawn_rows():
    stride = PACKED_TOKENS // 8
    return jnp.arange(8, dtype=jnp.int32) * stride + stride // 2 + 1


def shared_keys(key):
    start_offset = jnp.clip(jax.random.normal(key, (PACKED_TOKENS, KEY_VALUE_HEADS, HEAD_SIZE), jnp.float32), -6.0, 6.0)
    factor = jnp.exp(jax.random.uniform(jax.random.fold_in(key, 5), (PACKED_TOKENS, 1, 1), jnp.float32, math.log(0.3), 0.0))
    marked = jnp.zeros((PACKED_TOKENS,), jnp.float32).at[drawn_rows()].set(1.0)[:, None, None]
    factor = marked + (1.0 - marked) * factor
    return start_offset * factor


def draw_keys(key, part):
    start_offset = shared_keys(key)
    return start_offset.astype(jnp.bfloat16)


def draw_queries(key, part):
    key = jax.random.fold_in(key, 11)
    result = jnp.clip(jax.random.normal(key, (PACKED_TOKENS, QUERY_HEADS, HEAD_SIZE), jnp.float32), -6.0, 6.0)
    return result.astype(jnp.bfloat16)


def block_levels(key, extent, split, least, top_value):
    gain = 1.0
    for position, blocks in split:
        heights = jax.random.uniform(jax.random.fold_in(jax.random.fold_in(key, 6), position), (blocks,), jnp.float32, least / len(split), top_value / len(split))
        gain = gain * jnp.repeat(jnp.exp(heights), extent[position] // blocks).reshape((-1,) + (1,) * (len(extent) - 1 - position))
    return gain


def split_up(amount, total, bound, lean):
    loads = [(1 << 20) // math.isqrt(standing ** lean) + 1 for standing in range(2, amount + 1)]
    rest, given = total - bound - (amount - 1), [1] * (amount - 1)
    while rest > 0:
        free = [i for i in range(amount - 1) if given[i] < bound]
        pool, budget = sum([loads[i] for i in free]), rest
        for i in free:
            more = min(bound - given[i], max(1, budget * loads[i] // pool), rest)
            given[i] = given[i] + more
            rest = rest - more
    return np.array([bound] + given)


def uneven_parts(own_key, count, total, bound, lean):
    if count == 2:
        one = jax.random.randint(own_key, (), max(1, total - bound), min(bound, total - 1) + 1)
        return jnp.stack([one, total - one])
    tallies = jnp.asarray(split_up(count, total, bound, lean), jnp.int32)
    twos = (count - 1) // 2
    source_of, taker = tallies[1:1 + 2 * twos:2], tallies[2:2 + 2 * twos:2]
    margin = jnp.minimum(source_of - 1, bound - taker)
    passed = jax.random.randint(jax.random.fold_in(own_key, 1), (twos,), 0, 1 << 20) % (margin + 1)
    tallies = tallies.at[1:1 + 2 * twos:2].set(source_of - passed).at[2:2 + 2 * twos:2].set(taker + passed)
    return tallies[jax.random.permutation(jax.random.fold_in(own_key, 2), count)]


def gaussian(key, extent, scale, limit, split=(), kind=jnp.bfloat16):
    entries = jax.random.normal(key, extent, jnp.float32) * scale
    if len(split) > 0:
        entries = block_levels(key, extent, split, -0.22, 0.18) * entries
    return jnp.clip(entries, min=-limit, max=limit).astype(kind)


def setup_inputs(seed: int = 0) -> dict:
    key_of = jax.random.split(jax.random.key(seed), 8)
    return {
        "queries": draw_queries(jax.random.fold_in(key_of[7], 71), 0),
        "keys": draw_keys(jax.random.fold_in(key_of[7], 71), 0),
        "values": gaussian(key_of[2], (PACKED_TOKENS, KEY_VALUE_HEADS, HEAD_SIZE), 1.0, 6.0, ((0, 128),)),
        "out_states": gaussian(key_of[3], (PACKED_TOKENS, QUERY_HEADS, HEAD_SIZE), 1.0, 6.0, ((0, 128),)),
        "out_grads": gaussian(key_of[4], (PACKED_TOKENS, QUERY_HEADS, HEAD_SIZE), 1.0, 6.0, ((0, 128),)),
        "segment_ids": jnp.searchsorted(jnp.cumsum(uneven_parts(key_of[5], SEGS, PACKED_TOKENS, PACKED_TOKENS // 2, 2)), jnp.arange(PACKED_TOKENS), side="right").astype(jnp.int32),
        "span_position": jax.random.permutation(key_of[6], SPANS).astype(jnp.int32),
    }


def reference(queries, keys, values, out_states, out_grads, segment_ids, span_position):
    length = queries.shape[0]
    q_heads = queries.shape[1]
    kv_heads = keys.shape[1]
    width = queries.shape[2]
    group = q_heads // kv_heads
    scale = 1.0 / math.sqrt(width)
    stored = jnp.arange(length, dtype=jnp.int32)
    place = (span_position[stored // TOK_DEV] * TOK_DEV + stored % TOK_DEV).astype(jnp.int32)
    document = segment_ids[place]
    visible = (document[:, None] == document[None, :]) & (place[:, None] >= place[None, :])
    query_heads = queries.reshape(length, kv_heads, group, width).transpose(1, 2, 0, 3)
    state_heads = out_states.reshape(length, kv_heads, group, width).transpose(1, 2, 0, 3)
    grad_heads = out_grads.reshape(length, kv_heads, group, width).transpose(1, 2, 0, 3)
    key_heads = keys.transpose(1, 0, 2)
    value_heads = values.transpose(1, 0, 2)

    def one_kv(inputs):
        query_set, state_set, grad_set, key_mat, value_mat = inputs

        def one_head(carry, items):
            key_acc, value_acc = carry
            query_mat, state_mat, grad_mat = items
            scores = jnp.dot(query_mat, key_mat.T, preferred_element_type=jnp.float32) * scale
            top = lax.optimization_barrier(jnp.max(jnp.where(visible, scores, -jnp.inf), axis=-1))
            total = lax.optimization_barrier(jnp.sum(jnp.where(visible, jnp.exp(scores - top[:, None]), 0.0), axis=-1))
            lse = top + jnp.log(total)
            probs = jnp.where(visible, jnp.exp(scores - lse[:, None]), 0.0)
            dprobs = jnp.dot(grad_mat, value_mat.T, preferred_element_type=jnp.float32)
            delta = lax.optimization_barrier(jnp.sum(grad_mat.astype(jnp.float32) * state_mat.astype(jnp.float32), axis=-1))
            dscore = (probs * (dprobs - delta[:, None])).astype(jnp.bfloat16)
            query_part = scale * jnp.dot(dscore, key_mat, preferred_element_type=jnp.float32)
            key_acc = key_acc + jnp.dot(dscore.T, query_mat, preferred_element_type=jnp.float32)
            value_acc = value_acc + jnp.dot(probs.astype(jnp.bfloat16).T, grad_mat, preferred_element_type=jnp.float32)
            return ((key_acc, value_acc), query_part.astype(jnp.bfloat16))
        start = (jnp.zeros((length, width), jnp.float32), jnp.zeros((length, width), jnp.float32))
        (key_acc, value_acc), query_parts = lax.scan(one_head, start, (query_set, state_set, grad_set))
        return (query_parts, (scale * key_acc).astype(jnp.bfloat16), value_acc.astype(jnp.bfloat16))
    query_parts, key_parts, value_parts = lax.map(one_kv, (query_heads, state_heads, grad_heads, key_heads, value_heads))
    query_grad = query_parts.transpose(2, 0, 1, 3).reshape(length, q_heads, width)
    key_grad = key_parts.transpose(1, 0, 2)
    value_grad = value_parts.transpose(1, 0, 2)
    return (query_grad, key_grad, value_grad)
```

```python
import functools
import math

import jax
import jax.numpy as jnp
from jax import lax
from jax.experimental import pallas as pl
from jax.experimental.pallas import tpu as pltpu
from jax.sharding import PartitionSpec as P

AXES = ("head", "inner", "outer")
F32 = jnp.float32
BF16 = jnp.bfloat16
TOK = 32
GROUP = 8
ROWS = TOK * GROUP
KV0 = 2 * ROWS
DEL0 = KV0 + 2 * TOK
MSG = DEL0 + 16
TK = 256
LENGTH = 4096
PAD = LENGTH + TK
SPAN = 2048 + TOK + 128 + 2 * TK
LOW = -1e30
NT = (((1,), (1,)), ((), ()))


def linear(x, core, z, y_lo, y_hi):
    return (x * 2 + core) * 16 + (z * 2 + y_lo) * 2 + y_hi


def head_groups():
    return [
        [linear(g >> 1, core, z, (g & 1) ^ y_hi, y_hi) for g in range(8)]
        for core in range(2)
        for z in range(4)
        for y_hi in range(2)
    ]


def seq_groups():
    return [
        [linear(x, core, c >> 1, side ^ (c & 1), c & 1) for c in range(8)]
        for x in range(4)
        for core in range(2)
        for side in range(2)
    ]


def core_pairs():
    return [(i, i ^ 16) for i in range(128)]


def exchange(array, groups):
    return lax.all_to_all(
        array, AXES, split_axis=0, concat_axis=0, axis_index_groups=groups, tiled=True
    )


def dot(a, b):
    return jnp.dot(a, b, preferred_element_type=F32)


def pack_kernel(q_ref, g_ref, o_ref, k_ref, v_ref, out_ref):
    ones = jnp.ones((8, 128), BF16)
    for pair in range(4):
        cols = pl.ds(16 * pair, 16)
        q = q_ref[:, cols, :].astype(F32)
        g = g_ref[:, cols, :].astype(F32)
        prod = g * o_ref[:, cols, :].astype(F32)
        for half in range(2):
            j = 2 * pair + half
            sub = slice(8 * half, 8 * half + 8)
            out_ref[j, 0:ROWS, :] = q[:, sub, :].reshape(ROWS, 128).astype(BF16)
            out_ref[j, ROWS:KV0, :] = g[:, sub, :].reshape(ROWS, 128).astype(BF16)
            part = prod[:, sub, :].reshape(ROWS, 128)
            top = part.astype(BF16)
            rest = (part - top.astype(F32)).astype(BF16)
            delta = lax.dot_general(ones, top, NT, preferred_element_type=F32)
            delta = delta + lax.dot_general(ones, rest, NT, preferred_element_type=F32)
            delta = jnp.concatenate([delta[:, :128], delta[:, 128:]], axis=0)
            first = delta.astype(BF16).astype(F32)
            second = (delta - first).astype(BF16).astype(F32)
            third = delta - first - second
            row = lax.broadcasted_iota(jnp.int32, (16, 128), 0)
            packed = jnp.where(row % 8 == 0, first, jnp.where(row % 8 == 1, second, third))
            out_ref[j, DEL0:MSG, :] = packed.astype(BF16)
            out_ref[j, KV0 : KV0 + TOK, :] = k_ref[j]
            out_ref[j, KV0 + TOK : DEL0, :] = v_ref[j]


def stored_block(core, c, i):
    y_hi = c % 2
    return linear(i // 2, core, c // 2, (i + c) % 2, y_hi)


def attn_kernel(
    span_ref, start_ref, me_ref, msg_ref, kv0_ref, kv1_ref,
    dq_ref, part0_ref, part1_ref,
    k_s, kt_s, v_s, dk_s, dv_s, s_s,
):
    core = me_ref[0]
    mine = me_ref[1]
    scale = 1.0 / math.sqrt(128)
    factor = scale * math.log2(math.e)

    k_s[LENGTH:, :] = jnp.zeros((TK, 128), BF16)
    v_s[LENGTH:, :] = jnp.zeros((TK, 128), BF16)

    def place(n, _):
        c = n // 8
        i = n % 8
        for other, ref in ((0, kv0_ref), (1, kv1_ref)):
            who = (core + other) % 2
            at = pl.multiple_of(span_ref[stored_block(who, c, i)] * TOK, TOK)
            k_s[pl.ds(at, TOK), :] = ref[c, i, 0:TOK, :]
            v_s[pl.ds(at, TOK), :] = ref[c, i, TOK : 2 * TOK, :]
        return 0

    lax.fori_loop(0, 64, place, 0)

    def clear(n, _):
        at = pl.multiple_of(n * TK, TK)
        zero = jnp.zeros((TK, 128), F32)
        dk_s[pl.ds(at, TK), :] = zero
        dv_s[pl.ds(at, TK), :] = zero
        kt_s[:, pl.ds(at, TK)] = k_s[pl.ds(at, TK), :].T
        return 0

    lax.fori_loop(0, PAD // TK, clear, 0)

    def block(i, _):
        base = span_ref[stored_block(core, mine, i)] * TOK
        lane = lax.broadcasted_iota(jnp.int32, (1, ROWS), 1)
        place_q = base + lane // GROUP
        begin = jnp.zeros((1, ROWS), jnp.int32)
        low = jnp.int32(0)
        for s in range(1, 8):
            edge = start_ref[s]
            begin = jnp.where(place_q >= edge, jnp.maximum(begin, edge), begin)
            low = jnp.where(base >= edge, jnp.maximum(low, edge), low)
        first = low // 128 * 128
        tiles = (base + TOK - first + TK - 1) // TK
        q = msg_ref[i, 0:ROWS, :]
        grad = msg_ref[i, ROWS:KV0, :]
        tail = msg_ref[i, DEL0:MSG, :].astype(F32)
        halves = [tail[n : n + 1] + tail[n + 1 : n + 2] + tail[n + 2 : n + 3] for n in (0, 8)]
        delta = jnp.concatenate(halves, axis=1)

        def stats(t, carry):
            top, total = carry
            at = pl.multiple_of(first + t * TK, 128)
            keys = k_s[pl.ds(at, TK), :]
            s = lax.dot_general(keys, q, NT, preferred_element_type=F32) * factor
            pos = at + lax.broadcasted_iota(jnp.int32, (TK, ROWS), 0)
            s = jnp.where((pos <= place_q) & (pos >= begin), s, LOW)
            s_s[pl.ds(pl.multiple_of(t * TK, TK), TK), :] = s
            split = s.reshape(TK // 8, 8, ROWS)
            new = jnp.maximum(top, jnp.max(split, axis=0))
            total = total * jnp.exp2(top - new) + jnp.sum(jnp.exp2(split - new[None]), axis=0)
            return new, total

        top, total = lax.fori_loop(
            0, tiles, stats, (jnp.full((8, ROWS), LOW, F32), jnp.zeros((8, ROWS), F32))
        )
        peak = jnp.max(top, axis=0, keepdims=True)
        total = jnp.sum(total * jnp.exp2(top - peak), axis=0, keepdims=True)
        lse = peak + jnp.log2(total)

        def grads(t, acc):
            at = pl.multiple_of(first + t * TK, 128)
            p = jnp.exp2(s_s[pl.ds(pl.multiple_of(t * TK, TK), TK), :] - lse)
            dp = lax.dot_general(
                v_s[pl.ds(at, TK), :], grad, NT, preferred_element_type=F32
            )
            ds = (p * (dp - delta)).astype(BF16)
            dv_s[pl.ds(at, TK), :] += dot(p.astype(BF16), grad)
            dk_s[pl.ds(at, TK), :] += dot(ds, q)
            return acc + dot(kt_s[:, pl.ds(at, TK)], ds)

        acc = lax.fori_loop(0, tiles, grads, jnp.zeros((128, ROWS), F32))
        dq_ref[i, :, :] = (acc * scale).T.astype(BF16)
        return 0

    lax.fori_loop(0, 8, block, 0)

    def collect(n, _):
        c = n // 8
        i = n % 8
        for other, ref in ((0, part0_ref), (1, part1_ref)):
            who = (core + other) % 2
            at = pl.multiple_of(span_ref[stored_block(who, c, i)] * TOK, TOK)
            ref[c, i, 0:TOK, :] = (dk_s[pl.ds(at, TOK), :] * scale).astype(BF16)
            ref[c, i, TOK : 2 * TOK, :] = dv_s[pl.ds(at, TOK), :].astype(BF16)
        return 0

    lax.fori_loop(0, 64, collect, 0)


def vmem():
    return pl.BlockSpec(memory_space=pltpu.VMEM)


def smem():
    return pl.BlockSpec(memory_space=pltpu.SMEM)


def shards(queries, keys, values, out_states, out_grads, segment_ids, span_position):
    head = lax.axis_index("head")
    inner = lax.axis_index("inner")
    outer = lax.axis_index("outer")
    me = jnp.stack([head % 2, inner // 2 * 2 + outer]).astype(jnp.int32)
    starts = jnp.sum(
        segment_ids[None, :] < jnp.arange(8, dtype=jnp.int32)[:, None], axis=1, dtype=jnp.int32
    )
    message = pl.pallas_call(
        pack_kernel,
        out_shape=jax.ShapeDtypeStruct((8, MSG, 128), BF16),
        in_specs=[vmem()] * 5,
        out_specs=vmem(),
        compiler_params=pltpu.CompilerParams(vmem_limit_bytes=32 << 20),
        name="pack",
    )(queries, out_grads, out_states, keys.transpose(1, 0, 2), values.transpose(1, 0, 2))
    message = exchange(message, head_groups())
    kv_part = message[:, KV0:DEL0, :]
    kv_mine = exchange(
        jnp.broadcast_to(kv_part[None], (8, 8, 2 * TOK, 128)), seq_groups()
    )
    kv_other = lax.ppermute(kv_mine, AXES, core_pairs())
    kv_shape = jax.ShapeDtypeStruct((8, 8, 2 * TOK, 128), BF16)
    dq, part_mine, part_other = pl.pallas_call(
        attn_kernel,
        out_shape=(jax.ShapeDtypeStruct((8, ROWS, 128), BF16), kv_shape, kv_shape),
        in_specs=[smem()] * 3 + [vmem()] * 3,
        out_specs=(vmem(),) * 3,
        scratch_shapes=[
            pltpu.VMEM((PAD, 128), BF16),
            pltpu.VMEM((128, PAD), BF16),
            pltpu.VMEM((PAD, 128), BF16),
            pltpu.VMEM((PAD, 128), F32),
            pltpu.VMEM((PAD, 128), F32),
            pltpu.VMEM((SPAN, ROWS), F32),
        ],
        compiler_params=pltpu.CompilerParams(vmem_limit_bytes=48 << 20),
        name="attention",
    )(span_position, starts, me, message, kv_mine, kv_other)
    theirs = lax.ppermute(part_other, AXES, core_pairs())
    part = (part_mine.astype(F32) + theirs.astype(F32)).astype(BF16)
    part = exchange(part, seq_groups())
    total = jnp.sum(part.astype(F32), axis=0).astype(BF16)
    back = exchange(jnp.concatenate([dq, total], axis=1), head_groups())
    query_grad = back[:, :ROWS].reshape(8, TOK, GROUP, 128).transpose(1, 0, 2, 3)
    return (
        query_grad.reshape(TOK, 64, 128),
        back[:, ROWS : ROWS + TOK].transpose(1, 0, 2),
        back[:, ROWS + TOK :].transpose(1, 0, 2),
    )


def solution(mesh):
    spec = P(AXES, None, None)
    return jax.shard_map(
        shards,
        mesh=mesh,
        in_specs=(spec,) * 5 + (P(), P()),
        out_specs=(spec,) * 3,
        check_vma=False,
    )
```

```python
import math

import jax
import jax.numpy as jnp
from jax import lax
from jax.experimental import pallas as pl
from jax.experimental.pallas import tpu as pltpu
from jax.sharding import PartitionSpec as P

AXES = ("head", "inner", "outer")
F32 = jnp.float32
BF16 = jnp.bfloat16
I32 = jnp.int32
TOK = 32
HEADS = 64
MSG = 4 * TOK + 8
BACK = 3 * TOK
TK = 256
TQ = 256
BLOCKS = TQ // TOK
LENGTH = 4096
PAD = LENGTH + TK
LOW = -1e30
NT = (((1,), (1,)), ((), ()))


def linear(x, core, z, y_lo, y_hi):
    return (x * 2 + core) * 16 + (z * 2 + y_lo) * 2 + y_hi


def owner(core, rank):
    g = rank // 8
    c = rank % 8
    return linear(g // 2, core, c // 2, (g + c) % 2, c % 2)


def chip_groups():
    return [[owner(core, rank) for rank in range(64)] for core in range(2)]


def core_pairs():
    return [(i, i ^ 16) for i in range(128)]


def exchange(array):
    return lax.all_to_all(
        array, AXES, split_axis=0, concat_axis=0, axis_index_groups=chip_groups(), tiled=True
    )


def dot(a, b):
    return jnp.dot(a, b, preferred_element_type=F32)


def pack_kernel(q_hbm, g_hbm, o_hbm, k_hbm, v_hbm, out_ref, q_v, g_v, o_v, k_v, v_v, wide, sem):
    copies = []
    for n, (src, dst) in enumerate(
        ((g_hbm, g_v), (o_hbm, o_v), (q_hbm, q_v), (k_hbm, k_v), (v_hbm, v_v))
    ):
        copy = pltpu.make_async_copy(src, dst, sem.at[n])
        copy.start()
        copies.append(copy)
    copies[0].wait()
    copies[1].wait()
    lane = lax.broadcasted_iota(I32, (HEADS, 128), 1) % TOK
    ones = jnp.ones((128, 128), BF16)

    def token(t, delta):
        prod = g_v[t].astype(F32) * o_v[t].astype(F32)
        top = prod.astype(BF16)
        rest = (prod - top.astype(F32)).astype(BF16)
        return jnp.where(lane == t, dot(top, ones) + dot(rest, ones), delta)

    delta = lax.fori_loop(0, TOK, token, jnp.zeros((HEADS, 128), F32))
    first = delta.astype(BF16).astype(F32)
    second = (delta - first).astype(BF16).astype(F32)
    third = delta - first - second
    row = lax.broadcasted_iota(I32, (8, 128), 0)
    for h in range(HEADS):
        at = slice(h, h + 1)
        tile = jnp.where(row == 0, first[at], jnp.where(row == 1, second[at], third[at]))
        out_ref[h, 4 * TOK :, :] = tile.astype(BF16)
    for n, ref in ((1, g_v), (0, q_v)):
        if n == 0:
            copies[2].wait()
        wide[...] = ref[...].reshape(TOK * HEADS, 128).astype(F32)
        for h in range(HEADS):
            out_ref[h, n * TOK : n * TOK + TOK, :] = wide[pl.ds(h, TOK, HEADS), :].astype(BF16)
    for n, ref in ((2, k_v), (3, v_v)):
        copies[n + 1].wait()
        wide[0 : TOK * 8, :] = ref[...].reshape(TOK * 8, 128).astype(F32)
        for g in range(8):
            part = wide[pl.ds(g, TOK, 8), :].astype(BF16)
            for c in range(8):
                out_ref[g * 8 + c, n * TOK : n * TOK + TOK, :] = part


def attn_kernel(
    span_ref, start_ref, rank_ref, me_ref, msg_ref, kv_ref,
    dq_ref, mine_ref, other_ref,
    q_s, g_s, d_s, pos_s, from_s, k_s, kt_s, v_s, dk_s, dv_s, s_s,
):
    core = me_ref[0]
    scale = 1.0 / math.sqrt(128)
    factor = scale * math.log2(math.e)

    k_s[LENGTH:, :] = jnp.zeros((TK, 128), BF16)
    v_s[LENGTH:, :] = jnp.zeros((TK, 128), BF16)

    def place(r, _):
        block = owner(core, r)
        at = pl.multiple_of(span_ref[block] * TOK, TOK)
        k_s[pl.ds(at, TOK), :] = msg_ref[r, 2 * TOK : 3 * TOK, :]
        v_s[pl.ds(at, TOK), :] = msg_ref[r, 3 * TOK : 4 * TOK, :]
        slot = rank_ref[block // 32 * 16 + block % 16]
        pos_s[slot] = span_ref[block] * TOK
        from_s[slot] = r
        row = pl.multiple_of(slot * TOK, TOK)
        q_s[pl.ds(row, TOK), :] = msg_ref[r, 0:TOK, :]
        g_s[pl.ds(row, TOK), :] = msg_ref[r, TOK : 2 * TOK, :]
        d_s[pl.ds(pl.multiple_of(slot * 8, 8), 8), :] = msg_ref[r, 4 * TOK :, :].astype(F32)
        at = pl.multiple_of(span_ref[owner(1 - core, r)] * TOK, TOK)
        k_s[pl.ds(at, TOK), :] = kv_ref[r, 0:TOK, :]
        v_s[pl.ds(at, TOK), :] = kv_ref[r, TOK : 2 * TOK, :]
        return 0

    lax.fori_loop(0, 64, place, 0)

    def clear(n, _):
        at = pl.multiple_of(n * TK, TK)
        zero = jnp.zeros((TK, 128), F32)
        dk_s[pl.ds(at, TK), :] = zero
        dv_s[pl.ds(at, TK), :] = zero
        kt_s[:, pl.ds(at, TK)] = k_s[pl.ds(at, TK), :].T
        return 0

    lax.fori_loop(0, PAD // TK, clear, 0)

    lane = lax.broadcasted_iota(I32, (1, TQ), 1)
    sub = lax.broadcasted_iota(I32, (8, TQ), 0)
    step = lax.broadcasted_iota(I32, (TK // 8, 8, TQ), 0) * 8

    def tile(i, _):
        slot = i * BLOCKS
        lead = jnp.zeros((1, TQ), I32)
        parts = []
        for j in range(BLOCKS):
            lead = jnp.where(lane // TOK == j, pos_s[slot + j], lead)
            d = d_s[pl.ds(pl.multiple_of((slot + j) * 8, 8), 8), :]
            parts.append(d[0:1] + d[1:2] + d[2:3])
        small = lane[:, :128] // TOK
        sides = []
        for n in range(0, BLOCKS, 4):
            side = parts[n]
            for j in range(1, 4):
                side = jnp.where(small == j, parts[n + j], side)
            sides.append(side)
        delta = jnp.concatenate(sides, axis=1)
        place_q = lead + lane % TOK
        begin = jnp.zeros((1, TQ), I32)
        low = jnp.int32(0)
        base = pos_s[slot]
        for s in range(1, 8):
            edge = start_ref[s]
            begin = jnp.where(place_q >= edge, jnp.maximum(begin, edge), begin)
            low = jnp.where(base >= edge, jnp.maximum(low, edge), low)
        first = low // 128 * 128
        tiles = (pos_s[slot + BLOCKS - 1] + TOK - first + TK - 1) // TK
        rows = pl.ds(pl.multiple_of(slot * TOK, TQ), TQ)
        q = q_s[rows, :]
        grad = g_s[rows, :]

        def stats(t, carry):
            top, total = carry
            at = pl.multiple_of(first + t * TK, 128)
            s = lax.dot_general(k_s[pl.ds(at, TK), :], q, NT, preferred_element_type=F32)
            s = (s * factor).reshape(TK // 8, 8, TQ)
            upper = place_q - at - sub
            lower = begin - at - sub
            s = jnp.where((step <= upper[None]) & (step >= lower[None]), s, LOW)
            s_s[pl.ds(pl.multiple_of(t * TK, TK), TK), :] = s.reshape(TK, TQ)
            new = jnp.maximum(top, jnp.max(s, axis=0))
            total = total * jnp.exp2(top - new) + jnp.sum(jnp.exp2(s - new[None]), axis=0)
            return new, total

        top, total = lax.fori_loop(
            0, tiles, stats, (jnp.full((8, TQ), LOW, F32), jnp.zeros((8, TQ), F32))
        )
        peak = jnp.max(top, axis=0, keepdims=True)
        total = jnp.sum(total * jnp.exp2(top - peak), axis=0, keepdims=True)
        lse = peak + jnp.log2(total)

        def grads(t, acc):
            at = pl.multiple_of(first + t * TK, 128)
            p = jnp.exp2(s_s[pl.ds(pl.multiple_of(t * TK, TK), TK), :] - lse)
            dp = lax.dot_general(v_s[pl.ds(at, TK), :], grad, NT, preferred_element_type=F32)
            ds = (p * (dp - delta)).astype(BF16)
            dv_s[pl.ds(at, TK), :] += dot(p.astype(BF16), grad)
            dk_s[pl.ds(at, TK), :] += dot(ds, q)
            return acc + dot(kt_s[:, pl.ds(at, TK)], ds)

        acc = lax.fori_loop(0, tiles, grads, jnp.zeros((128, TQ), F32))
        out = (acc * scale).T.astype(BF16)
        for j in range(BLOCKS):
            dq_ref[from_s[slot + j], :, :] = out[j * TOK : j * TOK + TOK]
        return 0

    lax.fori_loop(0, 64 // BLOCKS, tile, 0)

    def collect(r, _):
        at = pl.multiple_of(span_ref[owner(core, r)] * TOK, TOK)
        mine_ref[r, 0:TOK, :] = dk_s[pl.ds(at, TOK), :] * scale
        mine_ref[r, TOK : 2 * TOK, :] = dv_s[pl.ds(at, TOK), :]
        at = pl.multiple_of(span_ref[owner(1 - core, r)] * TOK, TOK)
        other_ref[r, 0:TOK, :] = (dk_s[pl.ds(at, TOK), :] * scale).astype(BF16)
        other_ref[r, TOK : 2 * TOK, :] = dv_s[pl.ds(at, TOK), :].astype(BF16)
        return 0

    lax.fori_loop(0, 64, collect, 0)


def vmem():
    return pl.BlockSpec(memory_space=pltpu.VMEM)


def smem():
    return pl.BlockSpec(memory_space=pltpu.SMEM)


def hbm():
    return pl.BlockSpec(memory_space=pl.ANY)


def pack(queries, out_grads, out_states, keys, values):
    return pl.pallas_call(
        pack_kernel,
        out_shape=jax.ShapeDtypeStruct((HEADS, MSG, 128), BF16),
        in_specs=[hbm()] * 5,
        out_specs=vmem(),
        scratch_shapes=[pltpu.VMEM((TOK, HEADS, 128), BF16)] * 3
        + [pltpu.VMEM((TOK, 8, 128), BF16)] * 2
        + [pltpu.VMEM((TOK * HEADS, 128), F32), pltpu.SemaphoreType.DMA((5,))],
        compiler_params=pltpu.CompilerParams(vmem_limit_bytes=32 << 20),
        name="pack",
    )(queries, out_grads, out_states, keys, values)


def attention(span_position, starts, rank, me, message, kv_other):
    return pl.pallas_call(
        attn_kernel,
        out_shape=(
            jax.ShapeDtypeStruct((HEADS, TOK, 128), BF16),
            jax.ShapeDtypeStruct((HEADS, 2 * TOK, 128), F32),
            jax.ShapeDtypeStruct((HEADS, 2 * TOK, 128), BF16),
        ),
        in_specs=[smem()] * 4 + [vmem()] * 2,
        out_specs=(vmem(),) * 3,
        scratch_shapes=[
            pltpu.VMEM((64 * TOK, 128), BF16),
            pltpu.VMEM((64 * TOK, 128), BF16),
            pltpu.VMEM((64 * 8, 128), F32),
            pltpu.SMEM((64,), I32),
            pltpu.SMEM((64,), I32),
            pltpu.VMEM((PAD, 128), BF16),
            pltpu.VMEM((128, PAD), BF16),
            pltpu.VMEM((PAD, 128), BF16),
            pltpu.VMEM((PAD, 128), F32),
            pltpu.VMEM((PAD, 128), F32),
            pltpu.VMEM((PAD, TQ), F32),
        ],
        compiler_params=pltpu.CompilerParams(vmem_limit_bytes=48 << 20),
        name="attention",
    )(span_position, starts, rank, me, message, kv_other)


def shards(queries, keys, values, out_states, out_grads, segment_ids, span_position):
    core = lax.axis_index("head") % 2
    starts = jnp.sum(
        segment_ids[None, :] < jnp.arange(8, dtype=I32)[:, None], axis=1, dtype=I32
    )
    own = lax.dynamic_index_in_dim(span_position.reshape(4, 2, 16), core, 1, False).reshape(64)
    rank = jnp.sum(own[None, :] < own[:, None], axis=1, dtype=I32)
    message = exchange(pack(queries, out_grads, out_states, keys, values))
    kv_other = lax.ppermute(message[:, 2 * TOK : 4 * TOK, :], AXES, core_pairs())
    dq, mine, other = attention(
        span_position, starts, rank, core.astype(I32).reshape(1), message, kv_other
    )
    theirs = lax.ppermute(other, AXES, core_pairs())
    part = (mine + theirs.astype(F32)).astype(BF16)
    back = exchange(jnp.concatenate([dq, part], axis=1))
    sums = jnp.sum(back[:, TOK:].reshape(8, 8, 2, TOK, 128).astype(F32), axis=1).astype(BF16)
    return (
        back[:, :TOK].transpose(1, 0, 2),
        sums[:, 0].transpose(1, 0, 2),
        sums[:, 1].transpose(1, 0, 2),
    )


def solution(mesh):
    spec = P(AXES, None, None)
    return jax.shard_map(
        shards,
        mesh=mesh,
        in_specs=(spec,) * 5 + (P(), P()),
        out_specs=(spec,) * 3,
        check_vma=False,
    )
```

```python
import functools
import math

import jax
import jax.numpy as jnp
from jax import lax
from jax.experimental import pallas as pl
from jax.experimental.pallas import tpu as pltpu
from jax.sharding import PartitionSpec as P

AXES = ("head", "inner", "outer")
F32 = jnp.float32
BF16 = jnp.bfloat16
TOK = 32
GROUP = 8
ROWS = TOK * GROUP
KV0 = 2 * ROWS
DEL0 = KV0 + 2 * TOK
MSG = DEL0 + 16
TK = 256
LENGTH = 4096
PAD = LENGTH + 256
WIDE = 4
UNITS = 8 * (-(-(2048 + TOK + 128) // TK)) + WIDE
LOW = -1e30
NT = (((1,), (1,)), ((), ()))


def linear(x, core, z, y_lo, y_hi):
    return (x * 2 + core) * 16 + (z * 2 + y_lo) * 2 + y_hi


def head_groups():
    return [
        [linear(g >> 1, core, z, (g & 1) ^ y_hi, y_hi) for g in range(8)]
        for core in range(2)
        for z in range(4)
        for y_hi in range(2)
    ]


def seq_groups():
    return [
        [linear(x, core, c >> 1, side ^ (c & 1), c & 1) for c in range(8)]
        for x in range(4)
        for core in range(2)
        for side in range(2)
    ]


def core_pairs():
    return [(i, i ^ 16) for i in range(128)]


def exchange(array, groups):
    return lax.all_to_all(
        array, AXES, split_axis=0, concat_axis=0, axis_index_groups=groups, tiled=True
    )


def dot(a, b):
    return jnp.dot(a, b, preferred_element_type=F32)


def pack_kernel(q_ref, g_ref, o_ref, k_ref, v_ref, out_ref):
    ones = jnp.ones((8, 128), BF16)
    for pair in range(4):
        cols = pl.ds(16 * pair, 16)
        q = q_ref[:, cols, :].astype(F32)
        g = g_ref[:, cols, :].astype(F32)
        prod = g * o_ref[:, cols, :].astype(F32)
        for half in range(2):
            j = 2 * pair + half
            sub = slice(8 * half, 8 * half + 8)
            out_ref[j, 0:ROWS, :] = q[:, sub, :].reshape(ROWS, 128).astype(BF16)
            out_ref[j, ROWS:KV0, :] = g[:, sub, :].reshape(ROWS, 128).astype(BF16)
            part = prod[:, sub, :].reshape(ROWS, 128)
            top = part.astype(BF16)
            rest = (part - top.astype(F32)).astype(BF16)
            delta = lax.dot_general(ones, top, NT, preferred_element_type=F32)
            delta = delta + lax.dot_general(ones, rest, NT, preferred_element_type=F32)
            delta = jnp.concatenate([delta[:, :128], delta[:, 128:]], axis=0)
            first = delta.astype(BF16).astype(F32)
            second = (delta - first).astype(BF16).astype(F32)
            third = delta - first - second
            row = lax.broadcasted_iota(jnp.int32, (16, 128), 0)
            packed = jnp.where(row % 8 == 0, first, jnp.where(row % 8 == 1, second, third))
            out_ref[j, DEL0:MSG, :] = packed.astype(BF16)
            out_ref[j, KV0 : KV0 + TOK, :] = k_ref[j]
            out_ref[j, KV0 + TOK : DEL0, :] = v_ref[j]


def stored_block(core, c, i):
    y_hi = c % 2
    return linear(i // 2, core, c // 2, (i + c) % 2, y_hi)


def attn_kernel(
    span_ref, start_ref, me_ref, msg_ref, kv0_ref, kv1_ref,
    dq_ref, part0_ref, part1_ref,
    unit_q, unit_at, k_s, kt_s, v_s, qt_s, gt_s, d_s, hi_s, lo_s, dk_s, dv_s, dq_s, m_s, l_s, s_s,
):
    core = me_ref[0]
    mine = me_ref[1]
    scale = 1.0 / math.sqrt(128)
    factor = scale * math.log2(math.e)

    k_s[LENGTH:, :] = jnp.zeros((PAD - LENGTH, 128), BF16)
    v_s[LENGTH:, :] = jnp.zeros((PAD - LENGTH, 128), BF16)

    for c in range(8):
        for i in range(8):
            for other, ref in ((0, kv0_ref), (1, kv1_ref)):
                who = core if other == 0 else 1 - core
                at = pl.multiple_of(span_ref[stored_block(who, c, i)] * TOK, TOK)
                k_s[pl.ds(at, TOK), :] = ref[c, i, 0:TOK, :]
                v_s[pl.ds(at, TOK), :] = ref[c, i, TOK : 2 * TOK, :]
    zero = jnp.zeros((256, 128), F32)
    for at in range(0, PAD, 256):
        dk_s[at : at + 256, :] = zero
        dv_s[at : at + 256, :] = zero
        kt_s[:, at : at + 256] = k_s[at : at + 256, :].T

    lane = lax.broadcasted_iota(jnp.int32, (8, ROWS), 1)
    sub = lax.broadcasted_iota(jnp.int32, (8, ROWS), 0)
    step = lax.broadcasted_iota(jnp.int32, (TK // 8, 8, ROWS), 0) * 8
    count = jnp.int32(0)
    for i in range(8):
        base = span_ref[stored_block(core, mine, i)] * TOK
        place_q = base + lane // GROUP
        begin = jnp.zeros((8, ROWS), jnp.int32)
        low = jnp.int32(0)
        for s in range(1, 8):
            edge = start_ref[s]
            begin = jnp.where(place_q >= edge, jnp.maximum(begin, edge), begin)
            low = jnp.where(base >= edge, jnp.maximum(low, edge), low)
        hi_s[i] = place_q - sub
        lo_s[i] = begin - sub
        first = low // 128 * 128
        tiles = (base + TOK - first + TK - 1) // TK

        def enlist(t, _):
            unit_q[count + t] = i
            unit_at[count + t] = first + t * TK
            return 0

        lax.fori_loop(0, tiles, enlist, 0)
        count = count + tiles
        qt_s[i] = msg_ref[i, 0:ROWS, :].T
        gt_s[i] = msg_ref[i, ROWS:KV0, :].T
        tail = msg_ref[i, DEL0:MSG, :].astype(F32)
        halves = [tail[n : n + 1] + tail[n + 1 : n + 2] + tail[n + 2 : n + 3] for n in (0, 8)]
        d_s[i] = jnp.broadcast_to(jnp.concatenate(halves, axis=1), (8, ROWS))
        m_s[i] = jnp.full((8, ROWS), LOW, F32)
        l_s[i] = jnp.zeros((8, ROWS), F32)
        dq_s[i] = jnp.zeros((128, ROWS), F32)
    for n in range(WIDE - 1):
        unit_q[count + n] = 0
        unit_at[count + n] = LENGTH
    rounds = (count + WIDE - 1) // WIDE

    def stats(n, _):
        units = []
        for u in range(WIDE):
            i = unit_q[n * WIDE + u]
            at = pl.multiple_of(unit_at[n * WIDE + u], 128)
            units.append((i, at, dot(k_s[pl.ds(at, TK), :], qt_s[i])))
        results = []
        for u, (i, at, s) in enumerate(units):
            s = (s * factor).reshape(TK // 8, 8, ROWS)
            upper = hi_s[i] - at
            lower = lo_s[i] - at
            s = jnp.where((step <= upper[None]) & (step >= lower[None]), s, LOW)
            s_s[n * WIDE + u] = s.reshape(TK, ROWS)
            top = jnp.max(s, axis=0)
            results.append((i, top, jnp.sum(jnp.exp2(s - top[None]), axis=0)))
        for i, top, total in results:
            old = m_s[i]
            new = jnp.maximum(old, top)
            m_s[i] = new
            l_s[i] = l_s[i] * jnp.exp2(old - new) + total * jnp.exp2(top - new)
        return 0

    lax.fori_loop(0, rounds, stats, 0)
    for i in range(8):
        top = m_s[i]
        peak = jnp.max(top, axis=0, keepdims=True)
        total = jnp.sum(l_s[i] * jnp.exp2(top - peak), axis=0, keepdims=True)
        m_s[i] = jnp.broadcast_to(peak + jnp.log2(total), (8, ROWS))

    def grads(n, _):
        units = []
        for u in range(WIDE):
            i = unit_q[n * WIDE + u]
            at = pl.multiple_of(unit_at[n * WIDE + u], 128)
            units.append((i, at, dot(v_s[pl.ds(at, TK), :], gt_s[i])))
        results = []
        for u, (i, at, dp) in enumerate(units):
            s = s_s[n * WIDE + u].reshape(TK // 8, 8, ROWS)
            p = jnp.exp2(s - m_s[i][None])
            ds = p * (dp.reshape(TK // 8, 8, ROWS) - d_s[i][None])
            p = p.reshape(TK, ROWS).astype(BF16)
            ds = ds.reshape(TK, ROWS).astype(BF16)
            results.append((i, at, p, ds))
        for i, at, p, ds in results:
            dv_s[pl.ds(at, TK), :] += dot(p, msg_ref[i, ROWS:KV0, :])
            dk_s[pl.ds(at, TK), :] += dot(ds, msg_ref[i, 0:ROWS, :])
            dq_s[i] += dot(kt_s[:, pl.ds(at, TK)], ds)
        return 0

    lax.fori_loop(0, rounds, grads, 0)
    for i in range(8):
        dq_ref[i, :, :] = (dq_s[i] * scale).T.astype(BF16)

    for c in range(8):
        for i in range(8):
            for other, ref in ((0, part0_ref), (1, part1_ref)):
                who = core if other == 0 else 1 - core
                at = pl.multiple_of(span_ref[stored_block(who, c, i)] * TOK, TOK)
                ref[c, i, 0:TOK, :] = (dk_s[pl.ds(at, TOK), :] * scale).astype(BF16)
                ref[c, i, TOK : 2 * TOK, :] = dv_s[pl.ds(at, TOK), :].astype(BF16)


def vmem():
    return pl.BlockSpec(memory_space=pltpu.VMEM)


def smem():
    return pl.BlockSpec(memory_space=pltpu.SMEM)


def attention(span_position, starts, me, message, kv_mine, kv_other):
    kv_shape = jax.ShapeDtypeStruct((8, 8, 2 * TOK, 128), BF16)
    return pl.pallas_call(
        attn_kernel,
        out_shape=(jax.ShapeDtypeStruct((8, ROWS, 128), BF16), kv_shape, kv_shape),
        in_specs=[smem()] * 3 + [vmem()] * 3,
        out_specs=(vmem(),) * 3,
        scratch_shapes=[
            pltpu.SMEM((UNITS,), jnp.int32),
            pltpu.SMEM((UNITS,), jnp.int32),
            pltpu.VMEM((PAD, 128), BF16),
            pltpu.VMEM((128, PAD), BF16),
            pltpu.VMEM((PAD, 128), BF16),
            pltpu.VMEM((8, 128, ROWS), BF16),
            pltpu.VMEM((8, 128, ROWS), BF16),
            pltpu.VMEM((8, 8, ROWS), F32),
            pltpu.VMEM((8, 8, ROWS), jnp.int32),
            pltpu.VMEM((8, 8, ROWS), jnp.int32),
            pltpu.VMEM((PAD, 128), F32),
            pltpu.VMEM((PAD, 128), F32),
            pltpu.VMEM((8, 128, ROWS), F32),
            pltpu.VMEM((8, 8, ROWS), F32),
            pltpu.VMEM((8, 8, ROWS), F32),
            pltpu.VMEM((UNITS, TK, ROWS), F32),
        ],
        compiler_params=pltpu.CompilerParams(vmem_limit_bytes=56 << 20),
        name="attention",
    )(span_position, starts, me, message, kv_mine, kv_other)


def shards(queries, keys, values, out_states, out_grads, segment_ids, span_position):
    head = lax.axis_index("head")
    inner = lax.axis_index("inner")
    outer = lax.axis_index("outer")
    me = jnp.stack([head % 2, inner // 2 * 2 + outer]).astype(jnp.int32)
    starts = jnp.sum(
        segment_ids[None, :] < jnp.arange(8, dtype=jnp.int32)[:, None], axis=1, dtype=jnp.int32
    )
    message = pl.pallas_call(
        pack_kernel,
        out_shape=jax.ShapeDtypeStruct((8, MSG, 128), BF16),
        in_specs=[vmem()] * 5,
        out_specs=vmem(),
        compiler_params=pltpu.CompilerParams(vmem_limit_bytes=32 << 20),
        name="pack",
    )(queries, out_grads, out_states, keys.transpose(1, 0, 2), values.transpose(1, 0, 2))
    message = exchange(message, head_groups())
    kv_part = message[:, KV0:DEL0, :]
    kv_mine = exchange(
        jnp.broadcast_to(kv_part[None], (8, 8, 2 * TOK, 128)), seq_groups()
    )
    kv_other = lax.ppermute(kv_mine, AXES, core_pairs())
    dq, part_mine, part_other = attention(span_position, starts, me, message, kv_mine, kv_other)
    theirs = lax.ppermute(part_other, AXES, core_pairs())
    part = (part_mine.astype(F32) + theirs.astype(F32)).astype(BF16)
    part = exchange(part, seq_groups())
    total = jnp.sum(part.astype(F32), axis=0).astype(BF16)
    back = exchange(jnp.concatenate([dq, total], axis=1), head_groups())
    query_grad = back[:, :ROWS].reshape(8, TOK, GROUP, 128).transpose(1, 0, 2, 3)
    return (
        query_grad.reshape(TOK, 64, 128),
        back[:, ROWS : ROWS + TOK].transpose(1, 0, 2),
        back[:, ROWS + TOK :].transpose(1, 0, 2),
    )


def solution(mesh):
    spec = P(AXES, None, None)
    return jax.shard_map(
        shards,
        mesh=mesh,
        in_specs=(spec,) * 5 + (P(), P()),
        out_specs=(spec,) * 3,
        check_vma=False,
    )
```

```python
import functools
import math

import jax
import jax.numpy as jnp
from jax import lax
from jax.experimental import pallas as pl
from jax.experimental.pallas import tpu as pltpu
from jax.sharding import PartitionSpec as P

AXES = ("head", "inner", "outer")
F32 = jnp.float32
BF16 = jnp.bfloat16
TOK = 32
GROUP = 8
ROWS = TOK * GROUP
KV0 = 2 * ROWS
DEL0 = KV0 + 2 * TOK
MSG = DEL0 + 16
TK = 256
LENGTH = 4096
PAD = LENGTH + 256
WIDE = 4
LAG = 3
RING = LAG + 1
UNITS = 8 * (-(-(2048 + TOK + 128) // TK)) + WIDE
LOW = -1e30
NT = (((1,), (1,)), ((), ()))


def linear(x, core, z, y_lo, y_hi):
    return (x * 2 + core) * 16 + (z * 2 + y_lo) * 2 + y_hi


def head_groups():
    return [
        [linear(g >> 1, core, z, (g & 1) ^ y_hi, y_hi) for g in range(8)]
        for core in range(2)
        for z in range(4)
        for y_hi in range(2)
    ]


def seq_groups():
    return [
        [linear(x, core, c >> 1, side ^ (c & 1), c & 1) for c in range(8)]
        for x in range(4)
        for core in range(2)
        for side in range(2)
    ]


def core_pairs():
    return [(i, i ^ 16) for i in range(128)]


def exchange(array, groups):
    return lax.all_to_all(
        array, AXES, split_axis=0, concat_axis=0, axis_index_groups=groups, tiled=True
    )


def dot(a, b):
    return jnp.dot(a, b, preferred_element_type=F32)


def pack_kernel(q_hbm, g_hbm, o_hbm, k_hbm, v_hbm, out_ref, q_v, g_v, o_v, k_v, v_v, wide, sem):
    copies = []
    for n, (src, dst) in enumerate(
        ((g_hbm, g_v), (o_hbm, o_v), (q_hbm, q_v), (k_hbm, k_v), (v_hbm, v_v))
    ):
        copies.append(pltpu.make_async_copy(src, dst, sem.at[n]))
        copies[n].start()
    ones = jnp.ones((8, 128), BF16)
    copies[0].wait()
    copies[1].wait()
    for pair in range(4):
        cols = pl.ds(16 * pair, 16)
        g = g_v[:, cols, :].astype(F32)
        prod = g * o_v[:, cols, :].astype(F32)
        for half in range(2):
            j = 2 * pair + half
            sub = slice(8 * half, 8 * half + 8)
            out_ref[j, ROWS:KV0, :] = g[:, sub, :].reshape(ROWS, 128).astype(BF16)
            part = prod[:, sub, :].reshape(ROWS, 128)
            top = part.astype(BF16)
            rest = (part - top.astype(F32)).astype(BF16)
            delta = lax.dot_general(ones, top, NT, preferred_element_type=F32)
            delta = delta + lax.dot_general(ones, rest, NT, preferred_element_type=F32)
            delta = jnp.concatenate([delta[:, :128], delta[:, 128:]], axis=0)
            first = delta.astype(BF16).astype(F32)
            second = (delta - first).astype(BF16).astype(F32)
            third = delta - first - second
            row = lax.broadcasted_iota(jnp.int32, (16, 128), 0)
            packed = jnp.where(row % 8 == 0, first, jnp.where(row % 8 == 1, second, third))
            out_ref[j, DEL0:MSG, :] = packed.astype(BF16)
    copies[2].wait()
    for pair in range(4):
        q = q_v[:, pl.ds(16 * pair, 16), :].astype(F32)
        for half in range(2):
            sub = slice(8 * half, 8 * half + 8)
            out_ref[2 * pair + half, 0:ROWS, :] = q[:, sub, :].reshape(ROWS, 128).astype(BF16)
    for n, ref in ((0, k_v), (1, v_v)):
        copies[3 + n].wait()
        wide[...] = ref[...].reshape(ROWS, 128).astype(F32)
        for j in range(8):
            at = KV0 + n * TOK
            out_ref[j, at : at + TOK, :] = wide[pl.ds(j, TOK, 8), :].astype(BF16)


def unpack_kernel(back_ref, q_hbm, k_hbm, v_hbm, q_v, k_v, v_v, wide, sem):
    copies = []
    for n, (src, dst) in enumerate(((k_v, k_hbm), (v_v, v_hbm))):
        for j in range(8):
            at = ROWS + n * TOK
            wide[pl.ds(j, TOK, 8), :] = back_ref[j, at : at + TOK, :].astype(F32)
        src[...] = wide[...].reshape(TOK, 8, 128).astype(BF16)
        copies.append(pltpu.make_async_copy(src, dst, sem.at[n]))
        copies[-1].start()
    for pair in range(4):
        cols = pl.ds(16 * pair, 16)
        sides = [
            back_ref[2 * pair + half, 0:ROWS, :].astype(F32).reshape(TOK, 8, 128)
            for half in range(2)
        ]
        q_v[:, cols, :] = jnp.concatenate(sides, axis=1).astype(BF16)
        copies.append(
            pltpu.make_async_copy(q_v.at[:, cols, :], q_hbm.at[:, cols, :], sem.at[2 + pair])
        )
        copies[-1].start()
    for copy in copies:
        copy.wait()


def stored_block(core, c, i):
    y_hi = c % 2
    return linear(i // 2, core, c // 2, (i + c) % 2, y_hi)


def attn_kernel(
    span_ref, start_ref, me_ref, msg_ref, kv0_ref, kv1_ref,
    dq_ref, part0_ref, part1_ref,
    unit_q, unit_at, k_s, kt_s, v_s, qt_s, gt_s, d_s, hi_s, lo_s, dk_s, dv_s, dq_s, m_s, l_s, w_s, s_s,
):
    core = me_ref[0]
    mine = me_ref[1]
    scale = 1.0 / math.sqrt(128)
    factor = scale * math.log2(math.e)

    k_s[LENGTH:, :] = jnp.zeros((PAD - LENGTH, 128), BF16)
    v_s[LENGTH:, :] = jnp.zeros((PAD - LENGTH, 128), BF16)

    for c in range(8):
        for i in range(8):
            for other, ref in ((0, kv0_ref), (1, kv1_ref)):
                who = core if other == 0 else 1 - core
                at = pl.multiple_of(span_ref[stored_block(who, c, i)] * TOK, TOK)
                k_s[pl.ds(at, TOK), :] = ref[c, i, 0:TOK, :]
                v_s[pl.ds(at, TOK), :] = ref[c, i, TOK : 2 * TOK, :]
    zero = jnp.zeros((256, 128), F32)
    for at in range(0, PAD, 256):
        dk_s[at : at + 256, :] = zero
        dv_s[at : at + 256, :] = zero
        kt_s[:, at : at + 256] = k_s[at : at + 256, :].T

    lane = lax.broadcasted_iota(jnp.int32, (8, ROWS), 1)
    sub = lax.broadcasted_iota(jnp.int32, (8, ROWS), 0)
    step = lax.broadcasted_iota(jnp.int32, (TK // 8, 8, ROWS), 0) * 8
    count = jnp.int32(0)
    for i in range(8):
        base = span_ref[stored_block(core, mine, i)] * TOK
        place_q = base + lane // GROUP
        begin = jnp.zeros((8, ROWS), jnp.int32)
        low = jnp.int32(0)
        for s in range(1, 8):
            edge = start_ref[s]
            begin = jnp.where(place_q >= edge, jnp.maximum(begin, edge), begin)
            low = jnp.where(base >= edge, jnp.maximum(low, edge), low)
        hi_s[i] = place_q - sub
        lo_s[i] = begin - sub
        first = low // 128 * 128
        tiles = (base + TOK - first + TK - 1) // TK

        def enlist(t, _):
            unit_q[count + t] = i
            unit_at[count + t] = first + t * TK
            return 0

        lax.fori_loop(0, tiles, enlist, 0)
        count = count + tiles
        qt_s[i] = msg_ref[i, 0:ROWS, :].T
        gt_s[i] = msg_ref[i, ROWS:KV0, :].T
        tail = msg_ref[i, DEL0:MSG, :].astype(F32)
        halves = [tail[n : n + 1] + tail[n + 1 : n + 2] + tail[n + 2 : n + 3] for n in (0, 8)]
        d_s[i] = jnp.broadcast_to(jnp.concatenate(halves, axis=1), (8, ROWS))
        m_s[i] = jnp.full((8, ROWS), LOW, F32)
        l_s[i] = jnp.zeros((8, ROWS), F32)
        dq_s[i] = jnp.zeros((128, ROWS), F32)
    for n in range(WIDE - 1):
        unit_q[count + n] = 0
        unit_at[count + n] = LENGTH
    rounds = (count + WIDE - 1) // WIDE

    def units_of(n):
        units = []
        for u in range(WIDE):
            i = unit_q[n * WIDE + u]
            units.append((n % RING * WIDE + u, i, pl.multiple_of(unit_at[n * WIDE + u], 128)))
        return units

    def stats_dots(units):
        return [dot(k_s[pl.ds(at, TK), :], qt_s[i]) for _, i, at in units]

    def stats_rest(units, scores):
        results = []
        for (slot, i, at), s in zip(units, scores):
            s = (s * factor).reshape(TK // 8, 8, ROWS)
            upper = hi_s[i] - at
            lower = lo_s[i] - at
            s = jnp.where((step <= upper[None]) & (step >= lower[None]), s, LOW)
            top = jnp.max(s, axis=0)
            e = jnp.exp2(s - top[None])
            s_s[slot] = e.reshape(TK, ROWS)
            w_s[slot] = top
            results.append((i, top, jnp.sum(e, axis=0)))
        for i, top, total in results:
            old = m_s[i]
            new = jnp.maximum(old, top)
            m_s[i] = new
            l_s[i] = l_s[i] * jnp.exp2(old - new) + total * jnp.exp2(top - new)

    def grads_dots(units):
        return [dot(v_s[pl.ds(at, TK), :], gt_s[i]) for _, i, at in units]

    def grads_soft(units, dps):
        results = []
        for (slot, i, at), dp in zip(units, dps):
            top = m_s[i]
            peak = jnp.max(top, axis=0, keepdims=True)
            total = jnp.sum(l_s[i] * jnp.exp2(top - peak), axis=0, keepdims=True)
            weight = jnp.exp2(w_s[slot] - peak) / total
            p = s_s[slot].reshape(TK // 8, 8, ROWS) * weight[None]
            ds = p * (dp.reshape(TK // 8, 8, ROWS) - d_s[i][None])
            p = p.reshape(TK, ROWS).astype(BF16)
            results.append((i, at, p, ds.reshape(TK, ROWS).astype(BF16)))
        return results

    def grads_rest(results):
        for i, at, p, ds in results:
            dv_s[pl.ds(at, TK), :] += dot(p, msg_ref[i, ROWS:KV0, :])
            dk_s[pl.ds(at, TK), :] += dot(ds, msg_ref[i, 0:ROWS, :])
            dq_s[i] += dot(kt_s[:, pl.ds(at, TK)], ds)

    def ahead(n, _):
        for unit in units_of(n):
            stats_rest([unit], stats_dots([unit]))
        return 0

    def behind(n, _):
        units = units_of(n)
        grads_rest(grads_soft(units, grads_dots(units)))
        return 0

    def split(n, _):
        behind(n - LAG, 0)
        return ahead(n, 0)

    lax.fori_loop(0, jnp.minimum(rounds, LAG), ahead, 0)
    lax.fori_loop(LAG, rounds, split, 0)
    lax.fori_loop(jnp.maximum(rounds - LAG, 0), rounds, behind, 0)
    for i in range(8):
        dq_ref[i, :, :] = (dq_s[i] * scale).T.astype(BF16)

    for c in range(8):
        for i in range(8):
            for other, ref in ((0, part0_ref), (1, part1_ref)):
                who = core if other == 0 else 1 - core
                at = pl.multiple_of(span_ref[stored_block(who, c, i)] * TOK, TOK)
                ref[c, i, 0:TOK, :] = dk_s[pl.ds(at, TOK), :].astype(BF16)
                ref[c, i, TOK : 2 * TOK, :] = dv_s[pl.ds(at, TOK), :].astype(BF16)


def vmem():
    return pl.BlockSpec(memory_space=pltpu.VMEM)


def smem():
    return pl.BlockSpec(memory_space=pltpu.SMEM)


def hbm():
    return pl.BlockSpec(memory_space=pl.ANY)


def pack(queries, out_grads, out_states, keys, values):
    return pl.pallas_call(
        pack_kernel,
        out_shape=jax.ShapeDtypeStruct((8, MSG, 128), BF16),
        in_specs=[hbm()] * 5,
        out_specs=vmem(),
        scratch_shapes=[pltpu.VMEM((TOK, 64, 128), BF16)] * 3
        + [pltpu.VMEM((TOK, 8, 128), BF16)] * 2
        + [pltpu.VMEM((ROWS, 128), F32), pltpu.SemaphoreType.DMA((5,))],
        compiler_params=pltpu.CompilerParams(vmem_limit_bytes=58 << 20),
        name="pack",
    )(queries, out_grads, out_states, keys, values)


def unpack(back):
    small = jax.ShapeDtypeStruct((TOK, 8, 128), BF16)
    return pl.pallas_call(
        unpack_kernel,
        out_shape=(jax.ShapeDtypeStruct((TOK, 64, 128), BF16), small, small),
        in_specs=[vmem()],
        out_specs=(hbm(),) * 3,
        scratch_shapes=[pltpu.VMEM((TOK, 64, 128), BF16)]
        + [pltpu.VMEM((TOK, 8, 128), BF16)] * 2
        + [pltpu.VMEM((ROWS, 128), F32), pltpu.SemaphoreType.DMA((6,))],
        compiler_params=pltpu.CompilerParams(vmem_limit_bytes=58 << 20),
        name="unpack",
    )(back)


def attention(span_position, starts, me, message, kv_mine, kv_other):
    kv_shape = jax.ShapeDtypeStruct((8, 8, 2 * TOK, 128), BF16)
    return pl.pallas_call(
        attn_kernel,
        out_shape=(jax.ShapeDtypeStruct((8, ROWS, 128), BF16), kv_shape, kv_shape),
        in_specs=[smem()] * 3 + [vmem()] * 3,
        out_specs=(vmem(),) * 3,
        scratch_shapes=[
            pltpu.SMEM((UNITS,), jnp.int32),
            pltpu.SMEM((UNITS,), jnp.int32),
            pltpu.VMEM((PAD, 128), BF16),
            pltpu.VMEM((128, PAD), BF16),
            pltpu.VMEM((PAD, 128), BF16),
            pltpu.VMEM((8, 128, ROWS), BF16),
            pltpu.VMEM((8, 128, ROWS), BF16),
            pltpu.VMEM((8, 8, ROWS), F32),
            pltpu.VMEM((8, 8, ROWS), jnp.int32),
            pltpu.VMEM((8, 8, ROWS), jnp.int32),
            pltpu.VMEM((PAD, 128), F32),
            pltpu.VMEM((PAD, 128), F32),
            pltpu.VMEM((8, 128, ROWS), F32),
            pltpu.VMEM((8, 8, ROWS), F32),
            pltpu.VMEM((8, 8, ROWS), F32),
            pltpu.VMEM((RING * WIDE, 8, ROWS), F32),
            pltpu.VMEM((RING * WIDE, TK, ROWS), F32),
        ],
        compiler_params=pltpu.CompilerParams(vmem_limit_bytes=32 << 20),
        name="attention",
    )(span_position, starts, me, message, kv_mine, kv_other)


def shards(queries, keys, values, out_states, out_grads, segment_ids, span_position):
    head = lax.axis_index("head")
    inner = lax.axis_index("inner")
    outer = lax.axis_index("outer")
    me = jnp.stack([head % 2, inner // 2 * 2 + outer]).astype(jnp.int32)
    starts = jnp.sum(
        segment_ids[None, :] < jnp.arange(8, dtype=jnp.int32)[:, None], axis=1, dtype=jnp.int32
    )
    message = pack(queries, out_grads, out_states, keys, values)
    message = exchange(message, head_groups())
    kv_part = message[:, KV0:DEL0, :]
    kv_mine = exchange(
        jnp.broadcast_to(kv_part[None], (8, 8, 2 * TOK, 128)), seq_groups()
    )
    kv_other = lax.ppermute(kv_mine, AXES, core_pairs())
    dq, part_mine, part_other = attention(span_position, starts, me, message, kv_mine, kv_other)
    theirs = lax.ppermute(part_other, AXES, core_pairs())
    part = (part_mine.astype(F32) + theirs.astype(F32)).astype(BF16)
    part = exchange(part, seq_groups())
    total = jnp.sum(part.astype(F32), axis=0).reshape(8, 2, TOK, 128)
    factor = jnp.array([1.0 / math.sqrt(128), 1.0], F32).reshape(1, 2, 1, 1)
    total = (total * factor).astype(BF16).reshape(8, 2 * TOK, 128)
    return unpack(exchange(jnp.concatenate([dq, total], axis=1), head_groups()))


def solution(mesh):
    spec = P(AXES, None, None)
    return jax.shard_map(
        shards,
        mesh=mesh,
        in_specs=(spec,) * 5 + (P(), P()),
        out_specs=(spec,) * 3,
        check_vma=False,
    )
```

```python
import functools
import math

import jax
import jax.numpy as jnp
from jax import lax
from jax.experimental import pallas as pl
from jax.experimental.pallas import tpu as pltpu
from jax.sharding import PartitionSpec as P

AXES = ("head", "inner", "outer")
F32 = jnp.float32
BF16 = jnp.bfloat16
TOK = 32
GROUP = 8
ROWS = TOK * GROUP
DEL0 = 2 * ROWS
MSG = DEL0 + 16
PART = 2 * TOK
SHARE = ((3, 1, 6), (5, 4, 2))
LAST = 7
TK = 256
LENGTH = 4096
PAD = LENGTH + 256
WIDE = 4
LAG = 3
RING = LAG + 1
UNITS = 8 * (-(-(2048 + TOK + 128) // TK)) + WIDE
LOW = -1e30
NT = (((1,), (1,)), ((), ()))


def linear(x, core, z, y_lo, y_hi):
    return (x * 2 + core) * 16 + (z * 2 + y_lo) * 2 + y_hi


def head_groups():
    return [
        [linear(g >> 1, core, z, (g & 1) ^ y_hi, y_hi) for g in range(8)]
        for core in range(2)
        for z in range(4)
        for y_hi in range(2)
    ]


def core_pairs():
    return [(i, i ^ 16) for i in range(128)]


def seq_pairs(flips):
    pairs = []
    for x in range(4):
        for core in range(2):
            for z in range(4):
                for y in range(4):
                    e = flips[core]
                    pairs.append(
                        (
                            linear(x, core, z, y % 2, y // 2),
                            linear(x, core, z ^ (e >> 1), y % 2 ^ (e & 1), y // 2 ^ (e & 1)),
                        )
                    )
    return pairs


def to_core(array):
    return lax.ppermute(array, AXES, core_pairs())


def exchange(array):
    return lax.all_to_all(
        array, AXES, split_axis=0, concat_axis=0, axis_index_groups=head_groups(), tiled=True
    )


def dot(a, b):
    return jnp.dot(a, b, preferred_element_type=F32)


def pack_kv_kernel(k_hbm, v_hbm, out_ref, k_v, v_v, wide, sem):
    copies = []
    for n, (src, dst) in enumerate(((k_hbm, k_v), (v_hbm, v_v))):
        copies.append(pltpu.make_async_copy(src, dst, sem.at[n]))
        copies[n].start()
    for n, ref in ((0, k_v), (1, v_v)):
        copies[n].wait()
        wide[n] = ref[...].reshape(ROWS, 128).astype(F32)
        for j in range(8):
            out_ref[j, n * TOK : n * TOK + TOK, :] = wide[n, pl.ds(j, TOK, 8), :].astype(BF16)


def pack_q_kernel(q_hbm, g_hbm, o_hbm, out_ref, q_v, g_v, o_v, sem):
    copies = []
    for n, (src, dst) in enumerate(((g_hbm, g_v), (o_hbm, o_v), (q_hbm, q_v))):
        copies.append(pltpu.make_async_copy(src, dst, sem.at[n]))
        copies[n].start()
    ones = jnp.ones((8, 128), BF16)
    copies[0].wait()
    copies[1].wait()
    for pair in range(4):
        cols = pl.ds(16 * pair, 16)
        g = g_v[:, cols, :].astype(F32)
        prod = g * o_v[:, cols, :].astype(F32)
        for half in range(2):
            j = 2 * pair + half
            sub = slice(8 * half, 8 * half + 8)
            out_ref[j, ROWS:DEL0, :] = g[:, sub, :].reshape(ROWS, 128).astype(BF16)
            part = prod[:, sub, :].reshape(ROWS, 128)
            top = part.astype(BF16)
            rest = (part - top.astype(F32)).astype(BF16)
            delta = lax.dot_general(ones, top, NT, preferred_element_type=F32)
            delta = delta + lax.dot_general(ones, rest, NT, preferred_element_type=F32)
            delta = jnp.concatenate([delta[:, :128], delta[:, 128:]], axis=0)
            first = delta.astype(BF16).astype(F32)
            second = (delta - first).astype(BF16).astype(F32)
            third = delta - first - second
            row = lax.broadcasted_iota(jnp.int32, (16, 128), 0)
            packed = jnp.where(row % 8 == 0, first, jnp.where(row % 8 == 1, second, third))
            out_ref[j, DEL0:MSG, :] = packed.astype(BF16)
    copies[2].wait()
    for pair in range(4):
        q = q_v[:, pl.ds(16 * pair, 16), :].astype(F32)
        for half in range(2):
            sub = slice(8 * half, 8 * half + 8)
            out_ref[2 * pair + half, 0:ROWS, :] = q[:, sub, :].reshape(ROWS, 128).astype(BF16)


def unpack_q_kernel(back_ref, q_hbm, q_v, sem):
    copies = []
    for pair in range(4):
        cols = pl.ds(16 * pair, 16)
        sides = [
            back_ref[2 * pair + half].astype(F32).reshape(TOK, 8, 128) for half in range(2)
        ]
        q_v[:, cols, :] = jnp.concatenate(sides, axis=1).astype(BF16)
        copies.append(
            pltpu.make_async_copy(q_v.at[:, cols, :], q_hbm.at[:, cols, :], sem.at[pair])
        )
        copies[-1].start()
    for copy in copies:
        copy.wait()


def unpack_kv_kernel(back_ref, k_hbm, v_hbm, k_v, v_v, wide, sem):
    copies = []
    for n, (src, dst) in enumerate(((k_v, k_hbm), (v_v, v_hbm))):
        for j in range(8):
            wide[n, pl.ds(j, TOK, 8), :] = back_ref[j, n * TOK : n * TOK + TOK, :].astype(F32)
        src[...] = wide[n].reshape(TOK, 8, 128).astype(BF16)
        copies.append(pltpu.make_async_copy(src, dst, sem.at[n]))
        copies[-1].start()
    for copy in copies:
        copy.wait()


def stored_block(core, c, i):
    y_hi = c % 2
    return linear(i // 2, core, c // 2, (i + c) % 2, y_hi)


def chunk_places(span_ref, core, c):
    first = core * 16 + c // 2 * 4 + c % 2
    even = first + c % 2 * 2
    odd = first + 2 - c % 2 * 2
    return [
        pl.multiple_of(span_ref[i // 2 * 32 + (odd if i % 2 else even)] * TOK, TOK)
        for i in range(8)
    ]


def attn_kernel(
    span_ref, start_ref, me_ref, msg_ref,
    kv0_ref, kv1_ref, mine0_ref, mine1_ref, mine2_ref, mine3_ref,
    theirs0_ref, theirs1_ref, theirs2_ref, theirs3_ref,
    dq_ref, part0_ref, part1_ref,
    unit_q, unit_at, k_s, kt_s, v_s, qt_s, gt_s, d_s, hi_s, lo_s, dk_s, dv_s, dq_s, m_s, l_s, w_s, s_s,
):
    core = me_ref[0]
    mine = me_ref[1]
    scale = 1.0 / math.sqrt(128)
    factor = scale * math.log2(math.e)

    k_s[LENGTH:, :] = jnp.zeros((PAD - LENGTH, 128), BF16)
    v_s[LENGTH:, :] = jnp.zeros((PAD - LENGTH, 128), BF16)

    share = [jnp.where(core == 0, a, b) for a, b in zip(*SHARE)]
    share_other = [jnp.where(core == 0, b, a) for a, b in zip(*SHARE)]
    chunks = [(kv0_ref, None, core, 0), (kv1_ref, None, 1 - core, 0)]
    chunks += [(mine3_ref, None, core, LAST), (theirs3_ref, None, 1 - core, LAST)]
    for n, ref in enumerate((mine0_ref, mine1_ref, mine2_ref)):
        chunks += [(ref, 0, core, share[n]), (ref, 1, 1 - core, share[n])]
    for n, ref in enumerate((theirs0_ref, theirs1_ref, theirs2_ref)):
        chunks += [(ref, 0, 1 - core, share_other[n]), (ref, 1, core, share_other[n])]
    for ref, side, who, e in chunks:
        for i, at in enumerate(chunk_places(span_ref, who, mine ^ e)):
            part = ref[i] if side is None else ref[side, i]
            k_s[pl.ds(at, TOK), :] = part[0:TOK]
            v_s[pl.ds(at, TOK), :] = part[TOK:PART]
    zero = jnp.zeros((256, 128), F32)
    for at in range(0, PAD, 256):
        dk_s[at : at + 256, :] = zero
        dv_s[at : at + 256, :] = zero
        kt_s[:, at : at + 256] = k_s[at : at + 256, :].T

    lane = lax.broadcasted_iota(jnp.int32, (8, ROWS), 1)
    sub = lax.broadcasted_iota(jnp.int32, (8, ROWS), 0)
    step = lax.broadcasted_iota(jnp.int32, (TK // 8, 8, ROWS), 0) * 8
    count = jnp.int32(0)
    for i in range(8):
        base = span_ref[stored_block(core, mine, i)] * TOK
        place_q = base + lane // GROUP
        begin = jnp.zeros((8, ROWS), jnp.int32)
        low = jnp.int32(0)
        for s in range(1, 8):
            edge = start_ref[s]
            begin = jnp.where(place_q >= edge, jnp.maximum(begin, edge), begin)
            low = jnp.where(base >= edge, jnp.maximum(low, edge), low)
        hi_s[i] = place_q - sub
        lo_s[i] = begin - sub
        first = low // 128 * 128
        tiles = (base + TOK - first + TK - 1) // TK

        def enlist(t, _):
            unit_q[count + t] = i
            unit_at[count + t] = first + t * TK
            return 0

        lax.fori_loop(0, tiles, enlist, 0)
        count = count + tiles
        qt_s[i] = msg_ref[i, 0:ROWS, :].T
        gt_s[i] = msg_ref[i, ROWS:DEL0, :].T
        tail = msg_ref[i, DEL0:MSG, :].astype(F32)
        halves = [tail[n : n + 1] + tail[n + 1 : n + 2] + tail[n + 2 : n + 3] for n in (0, 8)]
        d_s[i] = jnp.broadcast_to(jnp.concatenate(halves, axis=1), (8, ROWS))
        m_s[i] = jnp.full((8, ROWS), LOW, F32)
        l_s[i] = jnp.zeros((8, ROWS), F32)
        dq_s[i] = jnp.zeros((128, ROWS), F32)
    for n in range(WIDE - 1):
        unit_q[count + n] = 0
        unit_at[count + n] = LENGTH
    rounds = (count + WIDE - 1) // WIDE

    def units_of(n):
        units = []
        for u in range(WIDE):
            i = unit_q[n * WIDE + u]
            units.append((n % RING * WIDE + u, i, pl.multiple_of(unit_at[n * WIDE + u], 128)))
        return units

    def stats_dots(units):
        return [dot(k_s[pl.ds(at, TK), :], qt_s[i]) for _, i, at in units]

    def stats_rest(units, scores):
        results = []
        for (slot, i, at), s in zip(units, scores):
            s = (s * factor).reshape(TK // 8, 8, ROWS)
            upper = hi_s[i] - at
            lower = lo_s[i] - at
            s = jnp.where((step <= upper[None]) & (step >= lower[None]), s, LOW)
            top = jnp.max(s, axis=0)
            e = jnp.exp2(s - top[None])
            s_s[slot] = e.reshape(TK, ROWS)
            w_s[slot] = top
            results.append((i, top, jnp.sum(e, axis=0)))
        for i, top, total in results:
            old = m_s[i]
            new = jnp.maximum(old, top)
            m_s[i] = new
            l_s[i] = l_s[i] * jnp.exp2(old - new) + total * jnp.exp2(top - new)

    def grads_dots(units):
        return [dot(v_s[pl.ds(at, TK), :], gt_s[i]) for _, i, at in units]

    def grads_soft(units, dps):
        results = []
        for (slot, i, at), dp in zip(units, dps):
            top = m_s[i]
            peak = jnp.max(top, axis=0, keepdims=True)
            total = jnp.sum(l_s[i] * jnp.exp2(top - peak), axis=0, keepdims=True)
            weight = jnp.exp2(w_s[slot] - peak) / total
            p = s_s[slot].reshape(TK // 8, 8, ROWS) * weight[None]
            ds = p * (dp.reshape(TK // 8, 8, ROWS) - d_s[i][None])
            p = p.reshape(TK, ROWS).astype(BF16)
            results.append((i, at, p, ds.reshape(TK, ROWS).astype(BF16)))
        return results

    def grads_rest(results):
        for i, at, p, ds in results:
            dv_s[pl.ds(at, TK), :] += dot(p, msg_ref[i, ROWS:DEL0, :])
            dk_s[pl.ds(at, TK), :] += dot(ds, msg_ref[i, 0:ROWS, :])
            dq_s[i] += dot(kt_s[:, pl.ds(at, TK)], ds)

    def ahead(n, _):
        for unit in units_of(n):
            stats_rest([unit], stats_dots([unit]))
        return 0

    def behind(n, _):
        units = units_of(n)
        grads_rest(grads_soft(units, grads_dots(units)))
        return 0

    def split(n, _):
        behind(n - LAG, 0)
        return ahead(n, 0)

    lax.fori_loop(0, jnp.minimum(rounds, LAG), ahead, 0)
    lax.fori_loop(LAG, rounds, split, 0)
    lax.fori_loop(jnp.maximum(rounds - LAG, 0), rounds, behind, 0)
    for i in range(8):
        dq_ref[i, :, :] = (dq_s[i] * scale).T.astype(BF16)

    for ref, me, flips in ((part0_ref, core, share), (part1_ref, 1 - core, share_other)):
        slots = [(who, e) for e in flips for who in (me, 1 - me)] + [(me, LAST), (me, 0)]
        for slot, (who, e) in enumerate(slots):
            for i, at in enumerate(chunk_places(span_ref, who, mine ^ e)):
                ref[slot, i, 0:TOK, :] = dk_s[pl.ds(at, TOK), :].astype(BF16)
                ref[slot, i, TOK:PART, :] = dv_s[pl.ds(at, TOK), :].astype(BF16)


def vmem():
    return pl.BlockSpec(memory_space=pltpu.VMEM)


def smem():
    return pl.BlockSpec(memory_space=pltpu.SMEM)


def hbm():
    return pl.BlockSpec(memory_space=pl.ANY)


def cost(megabytes):
    return pl.CostEstimate(flops=0, bytes_accessed=megabytes << 20, transcendentals=0)


def pack_kv(keys, values):
    return pl.pallas_call(
        pack_kv_kernel,
        out_shape=jax.ShapeDtypeStruct((8, PART, 128), BF16),
        in_specs=[hbm()] * 2,
        out_specs=vmem(),
        scratch_shapes=[pltpu.VMEM((TOK, 8, 128), BF16)] * 2
        + [pltpu.VMEM((2, ROWS, 128), F32), pltpu.SemaphoreType.DMA((2,))],
        compiler_params=pltpu.CompilerParams(vmem_limit_bytes=58 << 20),
        name="pack_kv",
    )(keys, values)


def pack_q(queries, out_grads, out_states):
    return pl.pallas_call(
        pack_q_kernel,
        out_shape=jax.ShapeDtypeStruct((8, MSG, 128), BF16),
        in_specs=[hbm()] * 3,
        out_specs=vmem(),
        scratch_shapes=[pltpu.VMEM((TOK, 64, 128), BF16)] * 3 + [pltpu.SemaphoreType.DMA((3,))],
        compiler_params=pltpu.CompilerParams(vmem_limit_bytes=58 << 20),
        cost_estimate=cost(8),
        name="pack_q",
    )(queries, out_grads, out_states)


def unpack_q(back):
    return pl.pallas_call(
        unpack_q_kernel,
        out_shape=jax.ShapeDtypeStruct((TOK, 64, 128), BF16),
        in_specs=[vmem()],
        out_specs=hbm(),
        scratch_shapes=[pltpu.VMEM((TOK, 64, 128), BF16), pltpu.SemaphoreType.DMA((4,))],
        compiler_params=pltpu.CompilerParams(vmem_limit_bytes=58 << 20),
        cost_estimate=cost(6),
        name="unpack_q",
    )(back)


def unpack_kv(back):
    small = jax.ShapeDtypeStruct((TOK, 8, 128), BF16)
    return pl.pallas_call(
        unpack_kv_kernel,
        out_shape=(small, small),
        in_specs=[vmem()],
        out_specs=(hbm(),) * 2,
        scratch_shapes=[pltpu.VMEM((TOK, 8, 128), BF16)] * 2
        + [pltpu.VMEM((2, ROWS, 128), F32), pltpu.SemaphoreType.DMA((2,))],
        compiler_params=pltpu.CompilerParams(vmem_limit_bytes=58 << 20),
        name="unpack_kv",
    )(back)


def attention(span_position, starts, me, message, parts):
    kv_shape = jax.ShapeDtypeStruct((8, 8, PART, 128), BF16)
    return pl.pallas_call(
        attn_kernel,
        out_shape=(jax.ShapeDtypeStruct((8, ROWS, 128), BF16), kv_shape, kv_shape),
        in_specs=[smem()] * 3 + [vmem()] * 11,
        out_specs=(vmem(),) * 3,
        scratch_shapes=[
            pltpu.SMEM((UNITS,), jnp.int32),
            pltpu.SMEM((UNITS,), jnp.int32),
            pltpu.VMEM((PAD, 128), BF16),
            pltpu.VMEM((128, PAD), BF16),
            pltpu.VMEM((PAD, 128), BF16),
            pltpu.VMEM((8, 128, ROWS), BF16),
            pltpu.VMEM((8, 128, ROWS), BF16),
            pltpu.VMEM((8, 8, ROWS), F32),
            pltpu.VMEM((8, 8, ROWS), jnp.int32),
            pltpu.VMEM((8, 8, ROWS), jnp.int32),
            pltpu.VMEM((PAD, 128), F32),
            pltpu.VMEM((PAD, 128), F32),
            pltpu.VMEM((8, 128, ROWS), F32),
            pltpu.VMEM((8, 8, ROWS), F32),
            pltpu.VMEM((8, 8, ROWS), F32),
            pltpu.VMEM((RING * WIDE, 8, ROWS), F32),
            pltpu.VMEM((RING * WIDE, TK, ROWS), F32),
        ],
        compiler_params=pltpu.CompilerParams(vmem_limit_bytes=32 << 20),
        name="attention",
    )(span_position, starts, me, message, *parts)


def shards(queries, keys, values, out_states, out_grads, segment_ids, span_position):
    head = lax.axis_index("head")
    inner = lax.axis_index("inner")
    outer = lax.axis_index("outer")
    me = jnp.stack([head % 2, inner // 2 * 2 + outer]).astype(jnp.int32)
    starts = jnp.sum(
        segment_ids[None, :] < jnp.arange(8, dtype=jnp.int32)[:, None], axis=1, dtype=jnp.int32
    )
    kv = exchange(pack_kv(keys, values))
    message = pack_q(queries, out_grads, out_states)
    kv, message = lax.optimization_barrier((kv, message))
    kv_theirs = to_core(kv)
    kv_theirs, message = lax.optimization_barrier((kv_theirs, message))
    message = exchange(message)
    both = jnp.stack([kv, kv_theirs])
    got = [lax.ppermute(both, AXES, seq_pairs(flips)) for flips in zip(*SHARE)]
    got.append(lax.ppermute(kv, AXES, seq_pairs((LAST, LAST))))
    parts = [kv, kv_theirs] + got + [to_core(part) for part in got]
    dq, mine, other = attention(span_position, starts, me, message, parts)
    part = (mine.astype(F32) + to_core(other).astype(F32)).astype(BF16)
    part, dq = lax.optimization_barrier((part, dq))
    dq = exchange(dq)
    got = [
        lax.ppermute(part[2 * n : 2 * n + 2], AXES, seq_pairs(flips)).astype(F32)
        for n, flips in enumerate(zip(*SHARE))
    ]
    last = lax.ppermute(part[6], AXES, seq_pairs((LAST, LAST)))
    total = part[7].astype(F32) + last.astype(F32) + got[0][0] + got[1][0] + got[2][0]
    give = got[0][1] + got[1][1] + got[2][1]
    total, give, dq = lax.optimization_barrier((total, give, dq))
    factor = jnp.array([1.0 / math.sqrt(128), 1.0], F32).reshape(1, 2, 1, 1)
    total = ((total + to_core(give)).reshape(8, 2, TOK, 128) * factor).astype(BF16)
    back = exchange(total.reshape(8, PART, 128))
    return (unpack_q(dq),) + tuple(unpack_kv(back))


def solution(mesh):
    spec = P(AXES, None, None)
    return jax.shard_map(
        shards,
        mesh=mesh,
        in_specs=(spec,) * 5 + (P(), P()),
        out_specs=(spec,) * 3,
        check_vma=False,
    )
```

```python
import functools
import math

import jax
import jax.numpy as jnp
from jax import lax
from jax.experimental import pallas as pl
from jax.experimental.pallas import tpu as pltpu
from jax.sharding import PartitionSpec as P

AXES = ("head", "inner", "outer")
F32 = jnp.float32
BF16 = jnp.bfloat16
TOK = 32
GROUP = 8
ROWS = TOK * GROUP
DEL0 = 2 * ROWS
MSG = DEL0 + 16
PART = 2 * TOK
SHARE = ((3, 1, 6), (5, 4, 2))
LAST = 7
TK = 256
LENGTH = 4096
PAD = LENGTH + 256
WIDE = 4
LAG = 3
RING = LAG + 1
UNITS = 8 * (-(-(2048 + TOK + 128) // TK)) + WIDE
LOW = -1e30
NT = (((1,), (1,)), ((), ()))


def linear(x, core, z, y_lo, y_hi):
    return (x * 2 + core) * 16 + (z * 2 + y_lo) * 2 + y_hi


def head_groups():
    return [
        [linear(g >> 1, core, z, (g & 1) ^ y_hi, y_hi) for g in range(8)]
        for core in range(2)
        for z in range(4)
        for y_hi in range(2)
    ]


def core_pairs():
    return [(i, i ^ 16) for i in range(128)]


def seq_pairs(flips):
    pairs = []
    for x in range(4):
        for core in range(2):
            for z in range(4):
                for y in range(4):
                    e = flips[core]
                    pairs.append(
                        (
                            linear(x, core, z, y % 2, y // 2),
                            linear(x, core, z ^ (e >> 1), y % 2 ^ (e & 1), y // 2 ^ (e & 1)),
                        )
                    )
    return pairs


def to_core(array):
    return lax.ppermute(array, AXES, core_pairs())


def exchange(array):
    return lax.all_to_all(
        array, AXES, split_axis=0, concat_axis=0, axis_index_groups=head_groups(), tiled=True
    )


def dot(a, b):
    return jnp.dot(a, b, preferred_element_type=F32)


def pack_kv_kernel(k_hbm, v_hbm, out_ref, k_v, v_v, wide, sem):
    copies = []
    for n, (src, dst) in enumerate(((k_hbm, k_v), (v_hbm, v_v))):
        copies.append(pltpu.make_async_copy(src, dst, sem.at[n]))
        copies[n].start()
    for n, ref in ((0, k_v), (1, v_v)):
        copies[n].wait()
        wide[n] = ref[...].reshape(ROWS, 128).astype(F32)
        for j in range(8):
            out_ref[j, n * TOK : n * TOK + TOK, :] = wide[n, pl.ds(j, TOK, 8), :].astype(BF16)


def pack_q_kernel(q_hbm, g_hbm, o_hbm, out_ref, q_v, g_v, o_v, sem):
    copies = []
    for n, (src, dst) in enumerate(((g_hbm, g_v), (o_hbm, o_v), (q_hbm, q_v))):
        copies.append(pltpu.make_async_copy(src, dst, sem.at[n]))
        copies[n].start()
    ones = jnp.ones((8, 128), BF16)
    copies[0].wait()
    copies[1].wait()
    for pair in range(4):
        cols = pl.ds(16 * pair, 16)
        g = g_v[:, cols, :].astype(F32)
        prod = g * o_v[:, cols, :].astype(F32)
        for half in range(2):
            j = 2 * pair + half
            sub = slice(8 * half, 8 * half + 8)
            out_ref[j, ROWS:DEL0, :] = g[:, sub, :].reshape(ROWS, 128).astype(BF16)
            part = prod[:, sub, :].reshape(ROWS, 128)
            top = part.astype(BF16)
            rest = (part - top.astype(F32)).astype(BF16)
            delta = lax.dot_general(ones, top, NT, preferred_element_type=F32)
            delta = delta + lax.dot_general(ones, rest, NT, preferred_element_type=F32)
            delta = jnp.concatenate([delta[:, :128], delta[:, 128:]], axis=0)
            first = delta.astype(BF16).astype(F32)
            second = (delta - first).astype(BF16).astype(F32)
            third = delta - first - second
            row = lax.broadcasted_iota(jnp.int32, (16, 128), 0)
            packed = jnp.where(row % 8 == 0, first, jnp.where(row % 8 == 1, second, third))
            out_ref[j, DEL0:MSG, :] = packed.astype(BF16)
    copies[2].wait()
    for pair in range(4):
        q = q_v[:, pl.ds(16 * pair, 16), :].astype(F32)
        for half in range(2):
            sub = slice(8 * half, 8 * half + 8)
            out_ref[2 * pair + half, 0:ROWS, :] = q[:, sub, :].reshape(ROWS, 128).astype(BF16)


def unpack_q_kernel(back_ref, q_hbm, q_v, sem):
    copies = []
    for pair in range(4):
        cols = pl.ds(16 * pair, 16)
        sides = [
            back_ref[2 * pair + half].astype(F32).reshape(TOK, 8, 128) for half in range(2)
        ]
        q_v[:, cols, :] = jnp.concatenate(sides, axis=1).astype(BF16)
        copies.append(
            pltpu.make_async_copy(q_v.at[:, cols, :], q_hbm.at[:, cols, :], sem.at[pair])
        )
        copies[-1].start()
    for copy in copies:
        copy.wait()


def unpack_kv_kernel(back_ref, k_hbm, v_hbm, k_v, v_v, wide, sem):
    copies = []
    for n, (src, dst) in enumerate(((k_v, k_hbm), (v_v, v_hbm))):
        for j in range(8):
            wide[n, pl.ds(j, TOK, 8), :] = back_ref[j, n * TOK : n * TOK + TOK, :].astype(F32)
        src[...] = wide[n].reshape(TOK, 8, 128).astype(BF16)
        copies.append(pltpu.make_async_copy(src, dst, sem.at[n]))
        copies[-1].start()
    for copy in copies:
        copy.wait()


def stored_block(core, c, i):
    y_hi = c % 2
    return linear(i // 2, core, c // 2, (i + c) % 2, y_hi)


def chunk_places(span_ref, core, c):
    first = core * 16 + c // 2 * 4 + c % 2
    even = first + c % 2 * 2
    odd = first + 2 - c % 2 * 2
    return [
        pl.multiple_of(span_ref[i // 2 * 32 + (odd if i % 2 else even)] * TOK, TOK)
        for i in range(8)
    ]


def attn_kernel(
    span_ref, start_ref, me_ref, msg_ref,
    kv0_ref, kv1_ref, mine0_ref, mine1_ref, mine2_ref, mine3_ref,
    theirs0_ref, theirs1_ref, theirs2_ref, theirs3_ref,
    dq_ref, part0_ref, part1_ref,
    unit_q, unit_at, k_s, kt_s, v_s, qt_s, gt_s, d_s, hi_s, lo_s, dk_s, dv_s, dq_s, m_s, l_s, w_s, s_s,
):
    core = me_ref[0]
    mine = me_ref[1]
    scale = 1.0 / math.sqrt(128)
    factor = scale * math.log2(math.e)

    k_s[LENGTH:, :] = jnp.zeros((PAD - LENGTH, 128), BF16)
    v_s[LENGTH:, :] = jnp.zeros((PAD - LENGTH, 128), BF16)

    share = [jnp.where(core == 0, a, b) for a, b in zip(*SHARE)]
    share_other = [jnp.where(core == 0, b, a) for a, b in zip(*SHARE)]
    chunks = [(kv0_ref, None, core, 0), (kv1_ref, None, 1 - core, 0)]
    chunks += [(mine3_ref, None, core, LAST), (theirs3_ref, None, 1 - core, LAST)]
    for n, ref in enumerate((mine0_ref, mine1_ref, mine2_ref)):
        chunks += [(ref, 0, core, share[n]), (ref, 1, 1 - core, share[n])]
    for n, ref in enumerate((theirs0_ref, theirs1_ref, theirs2_ref)):
        chunks += [(ref, 0, 1 - core, share_other[n]), (ref, 1, core, share_other[n])]
    for ref, side, who, e in chunks:
        for i, at in enumerate(chunk_places(span_ref, who, mine ^ e)):
            part = ref[i] if side is None else ref[side, i]
            k_s[pl.ds(at, TOK), :] = part[0:TOK]
            v_s[pl.ds(at, TOK), :] = part[TOK:PART]
    zero = jnp.zeros((256, 128), F32)
    for at in range(0, PAD, 256):
        dk_s[at : at + 256, :] = zero
        dv_s[at : at + 256, :] = zero
        kt_s[:, at : at + 256] = k_s[at : at + 256, :].T

    lane = lax.broadcasted_iota(jnp.int32, (8, ROWS), 1)
    sub = lax.broadcasted_iota(jnp.int32, (8, ROWS), 0)
    step = lax.broadcasted_iota(jnp.int32, (TK // 8, 8, ROWS), 0) * 8
    count = jnp.int32(0)
    for i in range(8):
        base = span_ref[stored_block(core, mine, i)] * TOK
        place_q = base + lane // GROUP
        begin = jnp.zeros((8, ROWS), jnp.int32)
        low = jnp.int32(0)
        for s in range(1, 8):
            edge = start_ref[s]
            begin = jnp.where(place_q >= edge, jnp.maximum(begin, edge), begin)
            low = jnp.where(base >= edge, jnp.maximum(low, edge), low)
        hi_s[i] = place_q - sub
        lo_s[i] = begin - sub
        first = low // 128 * 128
        tiles = (base + TOK - first + TK - 1) // TK

        def enlist(t, _):
            unit_q[count + t] = i
            unit_at[count + t] = first + t * TK
            return 0

        lax.fori_loop(0, tiles, enlist, 0)
        count = count + tiles
        qt_s[i] = msg_ref[i, 0:ROWS, :].T
        gt_s[i] = msg_ref[i, ROWS:DEL0, :].T
        tail = msg_ref[i, DEL0:MSG, :].astype(F32)
        halves = [tail[n : n + 1] + tail[n + 1 : n + 2] + tail[n + 2 : n + 3] for n in (0, 8)]
        d_s[i] = jnp.broadcast_to(jnp.concatenate(halves, axis=1), (8, ROWS))
        m_s[i] = jnp.full((8, ROWS), LOW, F32)
        l_s[i] = jnp.zeros((8, ROWS), F32)
        dq_s[i] = jnp.zeros((128, ROWS), F32)
    for n in range(WIDE - 1):
        unit_q[count + n] = 0
        unit_at[count + n] = LENGTH
    rounds = (count + WIDE - 1) // WIDE

    def units_of(n):
        units = []
        for u in range(WIDE):
            i = unit_q[n * WIDE + u]
            units.append((n % RING * WIDE + u, i, pl.multiple_of(unit_at[n * WIDE + u], 128)))
        return units

    def stats_dots(units):
        return [dot(k_s[pl.ds(at, TK), :], qt_s[i]) for _, i, at in units]

    def stats_rest(units, scores):
        results = []
        for (slot, i, at), s in zip(units, scores):
            s = (s * factor).reshape(TK // 8, 8, ROWS)
            upper = hi_s[i] - at
            span = (hi_s[i] - lo_s[i]).astype(jnp.uint32)
            back = (upper[None] - step).astype(jnp.uint32)
            s = jnp.where(back <= span[None], s, LOW)
            top = jnp.max(s, axis=0)
            e = jnp.exp2(s - top[None])
            s_s[slot] = e.reshape(TK, ROWS)
            w_s[slot] = top
            results.append((i, top, jnp.sum(e, axis=0)))
        for i, top, total in results:
            old = m_s[i]
            new = jnp.maximum(old, top)
            m_s[i] = new
            l_s[i] = l_s[i] * jnp.exp2(old - new) + total * jnp.exp2(top - new)

    def grads_dots(units):
        return [dot(v_s[pl.ds(at, TK), :], gt_s[i]) for _, i, at in units]

    def grads_soft(units, dps):
        results = []
        for (slot, i, at), dp in zip(units, dps):
            top = m_s[i]
            peak = jnp.max(top, axis=0, keepdims=True)
            total = jnp.sum(l_s[i] * jnp.exp2(top - peak), axis=0, keepdims=True)
            weight = jnp.exp2(w_s[slot] - peak) / total
            p = s_s[slot].reshape(TK // 8, 8, ROWS) * weight[None]
            ds = p * (dp.reshape(TK // 8, 8, ROWS) - d_s[i][None])
            p = p.reshape(TK, ROWS).astype(BF16)
            results.append((i, at, p, ds.reshape(TK, ROWS).astype(BF16)))
        return results

    def grads_rest(results):
        for i, at, p, ds in results:
            dv_s[pl.ds(at, TK), :] += dot(p, msg_ref[i, ROWS:DEL0, :])
            dk_s[pl.ds(at, TK), :] += dot(ds, msg_ref[i, 0:ROWS, :])
            dq_s[i] += dot(kt_s[:, pl.ds(at, TK)], ds)

    def ahead(n, _):
        for unit in units_of(n):
            stats_rest([unit], stats_dots([unit]))
        return 0

    def behind(n, _):
        units = units_of(n)
        grads_rest(grads_soft(units, grads_dots(units)))
        return 0

    def split(n, _):
        behind(n - LAG, 0)
        return ahead(n, 0)

    lax.fori_loop(0, jnp.minimum(rounds, LAG), ahead, 0)
    lax.fori_loop(LAG, rounds, split, 0)
    lax.fori_loop(jnp.maximum(rounds - LAG, 0), rounds, behind, 0)
    for i in range(8):
        dq_ref[i, :, :] = (dq_s[i] * scale).T.astype(BF16)

    for ref, me, flips in ((part0_ref, core, share), (part1_ref, 1 - core, share_other)):
        slots = [(who, e) for e in flips for who in (me, 1 - me)] + [(me, LAST), (me, 0)]
        for slot, (who, e) in enumerate(slots):
            for i, at in enumerate(chunk_places(span_ref, who, mine ^ e)):
                ref[slot, i, 0:TOK, :] = (dk_s[pl.ds(at, TOK), :] * scale).astype(BF16)
                ref[slot, i, TOK:PART, :] = dv_s[pl.ds(at, TOK), :].astype(BF16)


def vmem():
    return pl.BlockSpec(memory_space=pltpu.VMEM)


def smem():
    return pl.BlockSpec(memory_space=pltpu.SMEM)


def hbm():
    return pl.BlockSpec(memory_space=pl.ANY)


def cost(megabytes):
    return pl.CostEstimate(flops=0, bytes_accessed=megabytes << 20, transcendentals=0)


def pack_kv(keys, values):
    return pl.pallas_call(
        pack_kv_kernel,
        out_shape=jax.ShapeDtypeStruct((8, PART, 128), BF16),
        in_specs=[hbm()] * 2,
        out_specs=vmem(),
        scratch_shapes=[pltpu.VMEM((TOK, 8, 128), BF16)] * 2
        + [pltpu.VMEM((2, ROWS, 128), F32), pltpu.SemaphoreType.DMA((2,))],
        compiler_params=pltpu.CompilerParams(vmem_limit_bytes=58 << 20),
        name="pack_kv",
    )(keys, values)


def pack_q(queries, out_grads, out_states):
    return pl.pallas_call(
        pack_q_kernel,
        out_shape=jax.ShapeDtypeStruct((8, MSG, 128), BF16),
        in_specs=[hbm()] * 3,
        out_specs=vmem(),
        scratch_shapes=[pltpu.VMEM((TOK, 64, 128), BF16)] * 3 + [pltpu.SemaphoreType.DMA((3,))],
        compiler_params=pltpu.CompilerParams(vmem_limit_bytes=58 << 20),
        cost_estimate=cost(8),
        name="pack_q",
    )(queries, out_grads, out_states)


def unpack_q(back):
    return pl.pallas_call(
        unpack_q_kernel,
        out_shape=jax.ShapeDtypeStruct((TOK, 64, 128), BF16),
        in_specs=[vmem()],
        out_specs=hbm(),
        scratch_shapes=[pltpu.VMEM((TOK, 64, 128), BF16), pltpu.SemaphoreType.DMA((4,))],
        compiler_params=pltpu.CompilerParams(vmem_limit_bytes=58 << 20),
        cost_estimate=cost(6),
        name="unpack_q",
    )(back)


def unpack_kv(back):
    small = jax.ShapeDtypeStruct((TOK, 8, 128), BF16)
    return pl.pallas_call(
        unpack_kv_kernel,
        out_shape=(small, small),
        in_specs=[vmem()],
        out_specs=(hbm(),) * 2,
        scratch_shapes=[pltpu.VMEM((TOK, 8, 128), BF16)] * 2
        + [pltpu.VMEM((2, ROWS, 128), F32), pltpu.SemaphoreType.DMA((2,))],
        compiler_params=pltpu.CompilerParams(vmem_limit_bytes=58 << 20),
        name="unpack_kv",
    )(back)


def attention(span_position, starts, me, message, parts):
    kv_shape = jax.ShapeDtypeStruct((8, 8, PART, 128), BF16)
    return pl.pallas_call(
        attn_kernel,
        out_shape=(jax.ShapeDtypeStruct((8, ROWS, 128), BF16), kv_shape, kv_shape),
        in_specs=[smem()] * 3 + [vmem()] * 11,
        out_specs=(vmem(),) * 3,
        scratch_shapes=[
            pltpu.SMEM((UNITS,), jnp.int32),
            pltpu.SMEM((UNITS,), jnp.int32),
            pltpu.VMEM((PAD, 128), BF16),
            pltpu.VMEM((128, PAD), BF16),
            pltpu.VMEM((PAD, 128), BF16),
            pltpu.VMEM((8, 128, ROWS), BF16),
            pltpu.VMEM((8, 128, ROWS), BF16),
            pltpu.VMEM((8, 8, ROWS), F32),
            pltpu.VMEM((8, 8, ROWS), jnp.int32),
            pltpu.VMEM((8, 8, ROWS), jnp.int32),
            pltpu.VMEM((PAD, 128), F32),
            pltpu.VMEM((PAD, 128), F32),
            pltpu.VMEM((8, 128, ROWS), F32),
            pltpu.VMEM((8, 8, ROWS), F32),
            pltpu.VMEM((8, 8, ROWS), F32),
            pltpu.VMEM((RING * WIDE, 8, ROWS), F32),
            pltpu.VMEM((RING * WIDE, TK, ROWS), F32),
        ],
        compiler_params=pltpu.CompilerParams(vmem_limit_bytes=32 << 20),
        name="attention",
    )(span_position, starts, me, message, *parts)


def shards(queries, keys, values, out_states, out_grads, segment_ids, span_position):
    head = lax.axis_index("head")
    inner = lax.axis_index("inner")
    outer = lax.axis_index("outer")
    me = jnp.stack([head % 2, inner // 2 * 2 + outer]).astype(jnp.int32)
    starts = jnp.sum(
        segment_ids[None, :] < jnp.arange(8, dtype=jnp.int32)[:, None], axis=1, dtype=jnp.int32
    )
    kv = exchange(
        jnp.concatenate([keys.transpose(1, 0, 2), values.transpose(1, 0, 2)], axis=1)
    )
    message = pack_q(queries, out_grads, out_states)
    kv, message = lax.optimization_barrier((kv, message))
    kv_theirs = to_core(kv)
    kv_theirs, message = lax.optimization_barrier((kv_theirs, message))
    message = exchange(message)
    both = jnp.stack([kv, kv_theirs])
    got = [lax.ppermute(both, AXES, seq_pairs(flips)) for flips in zip(*SHARE)]
    got.append(lax.ppermute(kv, AXES, seq_pairs((LAST, LAST))))
    parts = [kv, kv_theirs] + got + [to_core(part) for part in got]
    dq, mine, other = attention(span_position, starts, me, message, parts)
    part = (mine.astype(F32) + to_core(other).astype(F32)).astype(BF16)
    dq = exchange(dq)
    got = [
        lax.ppermute(part[2 * n : 2 * n + 2], AXES, seq_pairs(flips)).astype(F32)
        for n, flips in enumerate(zip(*SHARE))
    ]
    last = lax.ppermute(part[6], AXES, seq_pairs((LAST, LAST)))
    total = part[7].astype(F32) + last.astype(F32) + got[0][0] + got[1][0] + got[2][0]
    give = got[0][1] + got[1][1] + got[2][1]
    total, give, dq = lax.optimization_barrier((total, give, dq))
    back = exchange((total + to_core(give)).astype(BF16))
    return (
        unpack_q(dq),
        back[:, :TOK].transpose(1, 0, 2),
        back[:, TOK:].transpose(1, 0, 2),
    )


def solution(mesh):
    spec = P(AXES, None, None)
    return jax.shard_map(
        shards,
        mesh=mesh,
        in_specs=(spec,) * 5 + (P(), P()),
        out_specs=(spec,) * 3,
        check_vma=False,
    )
```

```python
import functools
import math

import jax
import jax.numpy as jnp
from jax import lax
from jax.experimental import pallas as pl
from jax.experimental.pallas import tpu as pltpu
from jax.sharding import PartitionSpec as P

AXES = ("head", "inner", "outer")
F32 = jnp.float32
BF16 = jnp.bfloat16
TOK = 32
GROUP = 8
ROWS = TOK * GROUP
DEL0 = 2 * ROWS
MSG = DEL0 + 16
PART = 2 * TOK
SHARE = ((2, 6, 1), (5, 3, 4))
LAST = 7
TK = 256
LENGTH = 4096
PAD = LENGTH + 256
WIDE = 4
LAG = 3
RING = LAG + 1
UNITS = 8 * (-(-(2048 + TOK + 128) // TK)) + WIDE
LOW = -1e30
NT = (((1,), (1,)), ((), ()))


def linear(x, core, z, y_lo, y_hi):
    return (x * 2 + core) * 16 + (z * 2 + y_lo) * 2 + y_hi


def head_groups():
    return [
        [linear(g >> 1, core, z, (g & 1) ^ y_hi, y_hi) for g in range(8)]
        for core in range(2)
        for z in range(4)
        for y_hi in range(2)
    ]


def core_pairs():
    return [(i, i ^ 16) for i in range(128)]


def seq_pairs(flips):
    pairs = []
    for x in range(4):
        for core in range(2):
            for z in range(4):
                for y in range(4):
                    e = flips[core]
                    pairs.append(
                        (
                            linear(x, core, z, y % 2, y // 2),
                            linear(x, core, z ^ (e >> 1), y % 2 ^ (e & 1), y // 2 ^ (e & 1)),
                        )
                    )
    return pairs


def to_core(array):
    return lax.ppermute(array, AXES, core_pairs())


def exchange(array):
    return lax.all_to_all(
        array, AXES, split_axis=0, concat_axis=0, axis_index_groups=head_groups(), tiled=True
    )


def dot(a, b):
    return jnp.dot(a, b, preferred_element_type=F32)


def pack_kv_kernel(k_hbm, v_hbm, out_ref, k_v, v_v, wide, sem):
    copies = []
    for n, (src, dst) in enumerate(((k_hbm, k_v), (v_hbm, v_v))):
        copies.append(pltpu.make_async_copy(src, dst, sem.at[n]))
        copies[n].start()
    for n, ref in ((0, k_v), (1, v_v)):
        copies[n].wait()
        wide[n] = ref[...].reshape(ROWS, 128).astype(F32)
        for j in range(8):
            out_ref[j, n * TOK : n * TOK + TOK, :] = wide[n, pl.ds(j, TOK, 8), :].astype(BF16)


def pack_q_kernel(q_hbm, g_hbm, o_hbm, out_ref, q_v, g_v, o_v, sem):
    copies = []
    for n, (src, dst) in enumerate(((g_hbm, g_v), (o_hbm, o_v), (q_hbm, q_v))):
        copies.append(pltpu.make_async_copy(src, dst, sem.at[n]))
        copies[n].start()
    ones = jnp.ones((8, 128), BF16)
    copies[0].wait()
    copies[1].wait()
    for pair in range(4):
        cols = pl.ds(16 * pair, 16)
        g = g_v[:, cols, :].astype(F32)
        prod = g * o_v[:, cols, :].astype(F32)
        for half in range(2):
            j = 2 * pair + half
            sub = slice(8 * half, 8 * half + 8)
            out_ref[j, ROWS:DEL0, :] = g[:, sub, :].reshape(ROWS, 128).astype(BF16)
            part = prod[:, sub, :].reshape(ROWS, 128)
            top = part.astype(BF16)
            rest = (part - top.astype(F32)).astype(BF16)
            delta = lax.dot_general(ones, top, NT, preferred_element_type=F32)
            delta = delta + lax.dot_general(ones, rest, NT, preferred_element_type=F32)
            delta = jnp.concatenate([delta[:, :128], delta[:, 128:]], axis=0)
            first = delta.astype(BF16).astype(F32)
            second = (delta - first).astype(BF16).astype(F32)
            third = delta - first - second
            row = lax.broadcasted_iota(jnp.int32, (16, 128), 0)
            packed = jnp.where(row % 8 == 0, first, jnp.where(row % 8 == 1, second, third))
            out_ref[j, DEL0:MSG, :] = packed.astype(BF16)
    copies[2].wait()
    for pair in range(4):
        q = q_v[:, pl.ds(16 * pair, 16), :].astype(F32)
        for half in range(2):
            sub = slice(8 * half, 8 * half + 8)
            out_ref[2 * pair + half, 0:ROWS, :] = q[:, sub, :].reshape(ROWS, 128).astype(BF16)


def unpack_q_kernel(back_ref, q_hbm, q_v, sem):
    copies = []
    for pair in range(4):
        cols = pl.ds(16 * pair, 16)
        sides = [
            back_ref[2 * pair + half].astype(F32).reshape(TOK, 8, 128) for half in range(2)
        ]
        q_v[:, cols, :] = jnp.concatenate(sides, axis=1).astype(BF16)
        copies.append(
            pltpu.make_async_copy(q_v.at[:, cols, :], q_hbm.at[:, cols, :], sem.at[pair])
        )
        copies[-1].start()
    for copy in copies:
        copy.wait()


def unpack_kv_kernel(back_ref, k_hbm, v_hbm, k_v, v_v, wide, sem):
    copies = []
    for n, (src, dst) in enumerate(((k_v, k_hbm), (v_v, v_hbm))):
        for j in range(8):
            wide[n, pl.ds(j, TOK, 8), :] = back_ref[j, n * TOK : n * TOK + TOK, :].astype(F32)
        src[...] = wide[n].reshape(TOK, 8, 128).astype(BF16)
        copies.append(pltpu.make_async_copy(src, dst, sem.at[n]))
        copies[-1].start()
    for copy in copies:
        copy.wait()


def stored_block(core, c, i):
    y_hi = c % 2
    return linear(i // 2, core, c // 2, (i + c) % 2, y_hi)


def chunk_places(span_ref, core, c):
    first = core * 16 + c // 2 * 4 + c % 2
    even = first + c % 2 * 2
    odd = first + 2 - c % 2 * 2
    return [
        pl.multiple_of(span_ref[i // 2 * 32 + (odd if i % 2 else even)] * TOK, TOK)
        for i in range(8)
    ]


def attn_kernel(
    span_ref, start_ref, me_ref, msg_ref,
    kv0_ref, kv1_ref, mine0_ref, mine1_ref, mine2_ref, mine3_ref,
    theirs0_ref, theirs1_ref, theirs2_ref, theirs3_ref,
    dq_ref, part0_ref, part1_ref,
    unit_q, unit_at, k_s, kt_s, v_s, qt_s, gt_s, d_s, hi_s, lo_s, dk_s, dv_s, dq_s, m_s, l_s, w_s, s_s,
):
    core = me_ref[0]
    mine = me_ref[1]
    scale = 1.0 / math.sqrt(128)
    factor = scale * math.log2(math.e)

    k_s[LENGTH:, :] = jnp.zeros((PAD - LENGTH, 128), BF16)
    v_s[LENGTH:, :] = jnp.zeros((PAD - LENGTH, 128), BF16)

    share = [jnp.where(core == 0, a, b) for a, b in zip(*SHARE)]
    share_other = [jnp.where(core == 0, b, a) for a, b in zip(*SHARE)]
    chunks = [(kv0_ref, None, core, 0), (kv1_ref, None, 1 - core, 0)]
    chunks += [(mine3_ref, None, core, LAST), (theirs3_ref, None, 1 - core, LAST)]
    for n, ref in enumerate((mine0_ref, mine1_ref, mine2_ref)):
        chunks += [(ref, 0, core, share[n]), (ref, 1, 1 - core, share[n])]
    for n, ref in enumerate((theirs0_ref, theirs1_ref, theirs2_ref)):
        chunks += [(ref, 0, 1 - core, share_other[n]), (ref, 1, core, share_other[n])]
    for ref, side, who, e in chunks:
        for i, at in enumerate(chunk_places(span_ref, who, mine ^ e)):
            part = ref[i] if side is None else ref[side, i]
            k_s[pl.ds(at, TOK), :] = part[0:TOK]
            v_s[pl.ds(at, TOK), :] = part[TOK:PART]
    zero = jnp.zeros((256, 128), F32)
    for at in range(0, PAD, 256):
        dk_s[at : at + 256, :] = zero
        dv_s[at : at + 256, :] = zero
        kt_s[:, at : at + 256] = k_s[at : at + 256, :].T

    lane = lax.broadcasted_iota(jnp.int32, (8, ROWS), 1)
    sub = lax.broadcasted_iota(jnp.int32, (8, ROWS), 0)
    step = lax.broadcasted_iota(jnp.int32, (TK // 8, 8, ROWS), 0) * 8
    count = jnp.int32(0)
    for i in range(8):
        base = span_ref[stored_block(core, mine, i)] * TOK
        place_q = base + lane // GROUP
        begin = jnp.zeros((8, ROWS), jnp.int32)
        low = jnp.int32(0)
        for s in range(1, 8):
            edge = start_ref[s]
            begin = jnp.where(place_q >= edge, jnp.maximum(begin, edge), begin)
            low = jnp.where(base >= edge, jnp.maximum(low, edge), low)
        hi_s[i] = place_q - sub
        lo_s[i] = begin - sub
        first = low // 128 * 128
        tiles = (base + TOK - first + TK - 1) // TK

        def enlist(t, _):
            unit_q[count + t] = i
            unit_at[count + t] = first + t * TK
            return 0

        lax.fori_loop(0, tiles, enlist, 0)
        count = count + tiles
        qt_s[i] = msg_ref[i, 0:ROWS, :].T
        gt_s[i] = msg_ref[i, ROWS:DEL0, :].T
        tail = msg_ref[i, DEL0:MSG, :].astype(F32)
        halves = [tail[n : n + 1] + tail[n + 1 : n + 2] + tail[n + 2 : n + 3] for n in (0, 8)]
        d_s[i] = jnp.broadcast_to(jnp.concatenate(halves, axis=1), (8, ROWS))
        m_s[i] = jnp.full((8, ROWS), LOW, F32)
        l_s[i] = jnp.zeros((8, ROWS), F32)
        dq_s[i] = jnp.zeros((128, ROWS), F32)
    for n in range(WIDE - 1):
        unit_q[count + n] = 0
        unit_at[count + n] = LENGTH
    rounds = (count + WIDE - 1) // WIDE

    def units_of(n):
        units = []
        for u in range(WIDE):
            i = unit_q[n * WIDE + u]
            units.append((n % RING * WIDE + u, i, pl.multiple_of(unit_at[n * WIDE + u], 128)))
        return units

    def stats_dots(units):
        return [dot(k_s[pl.ds(at, TK), :], qt_s[i]) for _, i, at in units]

    def stats_rest(units, scores):
        results = []
        for (slot, i, at), s in zip(units, scores):
            s = (s * factor).reshape(TK // 8, 8, ROWS)
            upper = hi_s[i] - at
            span = (hi_s[i] - lo_s[i]).astype(jnp.uint32)
            back = (upper[None] - step).astype(jnp.uint32)
            s = jnp.where(back <= span[None], s, LOW)
            top = jnp.max(s, axis=0)
            e = jnp.exp2(s - top[None])
            s_s[slot] = e.reshape(TK, ROWS)
            w_s[slot] = top
            results.append((i, top, jnp.sum(e, axis=0)))
        for i, top, total in results:
            old = m_s[i]
            new = jnp.maximum(old, top)
            m_s[i] = new
            l_s[i] = l_s[i] * jnp.exp2(old - new) + total * jnp.exp2(top - new)

    def grads_dots(units):
        return [dot(v_s[pl.ds(at, TK), :], gt_s[i]) for _, i, at in units]

    def grads_soft(units, dps):
        results = []
        for (slot, i, at), dp in zip(units, dps):
            top = m_s[i]
            peak = jnp.max(top, axis=0, keepdims=True)
            total = jnp.sum(l_s[i] * jnp.exp2(top - peak), axis=0, keepdims=True)
            weight = jnp.exp2(w_s[slot] - peak) / total
            p = s_s[slot].reshape(TK // 8, 8, ROWS) * weight[None]
            ds = p * (dp.reshape(TK // 8, 8, ROWS) - d_s[i][None])
            p = p.reshape(TK, ROWS).astype(BF16)
            results.append((i, at, p, ds.reshape(TK, ROWS).astype(BF16)))
        return results

    def grads_rest(results):
        for i, at, p, ds in results:
            dv_s[pl.ds(at, TK), :] += dot(p, msg_ref[i, ROWS:DEL0, :])
            dk_s[pl.ds(at, TK), :] += dot(ds, msg_ref[i, 0:ROWS, :])
            dq_s[i] += dot(kt_s[:, pl.ds(at, TK)], ds)

    def ahead(n, _):
        for unit in units_of(n):
            stats_rest([unit], stats_dots([unit]))
        return 0

    def behind(n, _):
        units = units_of(n)
        grads_rest(grads_soft(units, grads_dots(units)))
        return 0

    def split(n, _):
        behind(n - LAG, 0)
        return ahead(n, 0)

    lax.fori_loop(0, jnp.minimum(rounds, LAG), ahead, 0)
    lax.fori_loop(LAG, rounds, split, 0)
    lax.fori_loop(jnp.maximum(rounds - LAG, 0), rounds, behind, 0)
    for i in range(8):
        dq_ref[i, :, :] = (dq_s[i] * scale).T.astype(BF16)

    for ref, me, flips in ((part0_ref, core, share), (part1_ref, 1 - core, share_other)):
        slots = [(who, e) for e in flips for who in (me, 1 - me)] + [(me, LAST), (me, 0)]
        for slot, (who, e) in enumerate(slots):
            for i, at in enumerate(chunk_places(span_ref, who, mine ^ e)):
                ref[slot, i, 0:TOK, :] = (dk_s[pl.ds(at, TOK), :] * scale).astype(BF16)
                ref[slot, i, TOK:PART, :] = dv_s[pl.ds(at, TOK), :].astype(BF16)


def vmem():
    return pl.BlockSpec(memory_space=pltpu.VMEM)


def smem():
    return pl.BlockSpec(memory_space=pltpu.SMEM)


def hbm():
    return pl.BlockSpec(memory_space=pl.ANY)


def cost(megabytes):
    return pl.CostEstimate(flops=0, bytes_accessed=megabytes << 20, transcendentals=0)


def pack_kv(keys, values):
    return pl.pallas_call(
        pack_kv_kernel,
        out_shape=jax.ShapeDtypeStruct((8, PART, 128), BF16),
        in_specs=[hbm()] * 2,
        out_specs=vmem(),
        scratch_shapes=[pltpu.VMEM((TOK, 8, 128), BF16)] * 2
        + [pltpu.VMEM((2, ROWS, 128), F32), pltpu.SemaphoreType.DMA((2,))],
        compiler_params=pltpu.CompilerParams(vmem_limit_bytes=58 << 20),
        name="pack_kv",
    )(keys, values)


def pack_q(queries, out_grads, out_states):
    return pl.pallas_call(
        pack_q_kernel,
        out_shape=jax.ShapeDtypeStruct((8, MSG, 128), BF16),
        in_specs=[hbm()] * 3,
        out_specs=vmem(),
        scratch_shapes=[pltpu.VMEM((TOK, 64, 128), BF16)] * 3 + [pltpu.SemaphoreType.DMA((3,))],
        compiler_params=pltpu.CompilerParams(vmem_limit_bytes=58 << 20),
        cost_estimate=cost(8),
        name="pack_q",
    )(queries, out_grads, out_states)


def unpack_q(back):
    return pl.pallas_call(
        unpack_q_kernel,
        out_shape=jax.ShapeDtypeStruct((TOK, 64, 128), BF16),
        in_specs=[vmem()],
        out_specs=hbm(),
        scratch_shapes=[pltpu.VMEM((TOK, 64, 128), BF16), pltpu.SemaphoreType.DMA((4,))],
        compiler_params=pltpu.CompilerParams(vmem_limit_bytes=58 << 20),
        cost_estimate=cost(6),
        name="unpack_q",
    )(back)


def unpack_kv(back):
    small = jax.ShapeDtypeStruct((TOK, 8, 128), BF16)
    return pl.pallas_call(
        unpack_kv_kernel,
        out_shape=(small, small),
        in_specs=[vmem()],
        out_specs=(hbm(),) * 2,
        scratch_shapes=[pltpu.VMEM((TOK, 8, 128), BF16)] * 2
        + [pltpu.VMEM((2, ROWS, 128), F32), pltpu.SemaphoreType.DMA((2,))],
        compiler_params=pltpu.CompilerParams(vmem_limit_bytes=58 << 20),
        name="unpack_kv",
    )(back)


def attention(span_position, starts, me, message, parts):
    kv_shape = jax.ShapeDtypeStruct((8, 8, PART, 128), BF16)
    return pl.pallas_call(
        attn_kernel,
        out_shape=(jax.ShapeDtypeStruct((8, ROWS, 128), BF16), kv_shape, kv_shape),
        in_specs=[smem()] * 3 + [vmem()] * 11,
        out_specs=(vmem(),) * 3,
        scratch_shapes=[
            pltpu.SMEM((UNITS,), jnp.int32),
            pltpu.SMEM((UNITS,), jnp.int32),
            pltpu.VMEM((PAD, 128), BF16),
            pltpu.VMEM((128, PAD), BF16),
            pltpu.VMEM((PAD, 128), BF16),
            pltpu.VMEM((8, 128, ROWS), BF16),
            pltpu.VMEM((8, 128, ROWS), BF16),
            pltpu.VMEM((8, 8, ROWS), F32),
            pltpu.VMEM((8, 8, ROWS), jnp.int32),
            pltpu.VMEM((8, 8, ROWS), jnp.int32),
            pltpu.VMEM((PAD, 128), F32),
            pltpu.VMEM((PAD, 128), F32),
            pltpu.VMEM((8, 128, ROWS), F32),
            pltpu.VMEM((8, 8, ROWS), F32),
            pltpu.VMEM((8, 8, ROWS), F32),
            pltpu.VMEM((RING * WIDE, 8, ROWS), F32),
            pltpu.VMEM((RING * WIDE, TK, ROWS), F32),
        ],
        compiler_params=pltpu.CompilerParams(vmem_limit_bytes=32 << 20),
        name="attention",
    )(span_position, starts, me, message, *parts)


def shards(queries, keys, values, out_states, out_grads, segment_ids, span_position):
    head = lax.axis_index("head")
    inner = lax.axis_index("inner")
    outer = lax.axis_index("outer")
    me = jnp.stack([head % 2, inner // 2 * 2 + outer]).astype(jnp.int32)
    starts = jnp.sum(
        segment_ids[None, :] < jnp.arange(8, dtype=jnp.int32)[:, None], axis=1, dtype=jnp.int32
    )
    kv = exchange(
        jnp.concatenate([keys.transpose(1, 0, 2), values.transpose(1, 0, 2)], axis=1)
    )
    message = pack_q(queries, out_grads, out_states)
    kv, message = lax.optimization_barrier((kv, message))
    kv_theirs = to_core(kv)
    kv_theirs, message = lax.optimization_barrier((kv_theirs, message))
    message = exchange(message)
    both = jnp.stack([kv, kv_theirs])
    got = [lax.ppermute(both, AXES, seq_pairs(flips)) for flips in zip(*SHARE)]
    got.append(lax.ppermute(kv, AXES, seq_pairs((LAST, LAST))))
    parts = [kv, kv_theirs] + got + [to_core(part) for part in got]
    dq, mine, other = attention(span_position, starts, me, message, parts)
    part = (mine.astype(F32) + to_core(other).astype(F32)).astype(BF16)
    dq = exchange(dq)
    got = [
        lax.ppermute(part[2 * n : 2 * n + 2], AXES, seq_pairs(flips)).astype(F32)
        for n, flips in enumerate(zip(*SHARE))
    ]
    last = lax.ppermute(part[6], AXES, seq_pairs((LAST, LAST)))
    total = part[7].astype(F32) + last.astype(F32) + got[0][0] + got[1][0] + got[2][0]
    give = got[0][1] + got[1][1] + got[2][1]
    total, give, dq = lax.optimization_barrier((total, give, dq))
    back = exchange((total + to_core(give)).astype(BF16))
    return (
        unpack_q(dq),
        back[:, :TOK].transpose(1, 0, 2),
        back[:, TOK:].transpose(1, 0, 2),
    )


def solution(mesh):
    spec = P(AXES, None, None)
    return jax.shard_map(
        shards,
        mesh=mesh,
        in_specs=(spec,) * 5 + (P(), P()),
        out_specs=(spec,) * 3,
        check_vma=False,
    )
```

```python
import functools
import math

import jax
import jax.numpy as jnp
from jax import lax
from jax.experimental import pallas as pl
from jax.experimental.pallas import tpu as pltpu
from jax.sharding import PartitionSpec as P

AXES = ("head", "inner", "outer")
F32 = jnp.float32
BF16 = jnp.bfloat16
TOK = 32
GROUP = 8
ROWS = TOK * GROUP
DEL0 = 2 * ROWS
MSG = DEL0 + 16
PART = 2 * TOK
SHARE = ((2, 6, 3), (5, 1, 4))
LAST = 7
TK = 256
LENGTH = 4096
PAD = LENGTH + 256
WIDE = 4
LAG = 3
RING = LAG + 1
UNITS = 8 * (-(-(2048 + TOK + 128) // TK)) + WIDE
LOW = -1e30
NT = (((1,), (1,)), ((), ()))


def linear(x, core, z, y_lo, y_hi):
    return (x * 2 + core) * 16 + (z * 2 + y_lo) * 2 + y_hi


def head_groups():
    return [
        [linear(g >> 1, core, z, (g & 1) ^ y_hi, y_hi) for g in range(8)]
        for core in range(2)
        for z in range(4)
        for y_hi in range(2)
    ]


def core_pairs():
    return [(i, i ^ 16) for i in range(128)]


def seq_pairs(flips):
    pairs = []
    for x in range(4):
        for core in range(2):
            for z in range(4):
                for y in range(4):
                    e = flips[core]
                    pairs.append(
                        (
                            linear(x, core, z, y % 2, y // 2),
                            linear(x, core, z ^ (e >> 1), y % 2 ^ (e & 1), y // 2 ^ (e & 1)),
                        )
                    )
    return pairs


def to_core(array):
    return lax.ppermute(array, AXES, core_pairs())


def exchange(array):
    return lax.all_to_all(
        array, AXES, split_axis=0, concat_axis=0, axis_index_groups=head_groups(), tiled=True
    )


def dot(a, b):
    return jnp.dot(a, b, preferred_element_type=F32)


def pack_kv_kernel(k_hbm, v_hbm, out_ref, k_v, v_v, wide, sem):
    copies = []
    for n, (src, dst) in enumerate(((k_hbm, k_v), (v_hbm, v_v))):
        copies.append(pltpu.make_async_copy(src, dst, sem.at[n]))
        copies[n].start()
    for n, ref in ((0, k_v), (1, v_v)):
        copies[n].wait()
        wide[n] = ref[...].reshape(ROWS, 128).astype(F32)
        for j in range(8):
            out_ref[j, n * TOK : n * TOK + TOK, :] = wide[n, pl.ds(j, TOK, 8), :].astype(BF16)


def pack_q_kernel(q_hbm, g_hbm, o_hbm, out_ref, q_v, g_v, o_v, sem):
    copies = []
    for n, (src, dst) in enumerate(((g_hbm, g_v), (o_hbm, o_v), (q_hbm, q_v))):
        copies.append(pltpu.make_async_copy(src, dst, sem.at[n]))
        copies[n].start()
    ones = jnp.ones((8, 128), BF16)
    copies[0].wait()
    copies[1].wait()
    for pair in range(4):
        cols = pl.ds(16 * pair, 16)
        g = g_v[:, cols, :].astype(F32)
        prod = g * o_v[:, cols, :].astype(F32)
        for half in range(2):
            j = 2 * pair + half
            sub = slice(8 * half, 8 * half + 8)
            out_ref[j, ROWS:DEL0, :] = g[:, sub, :].reshape(ROWS, 128).astype(BF16)
            part = prod[:, sub, :].reshape(ROWS, 128)
            top = part.astype(BF16)
            rest = (part - top.astype(F32)).astype(BF16)
            delta = lax.dot_general(ones, top, NT, preferred_element_type=F32)
            delta = delta + lax.dot_general(ones, rest, NT, preferred_element_type=F32)
            delta = jnp.concatenate([delta[:, :128], delta[:, 128:]], axis=0)
            first = delta.astype(BF16).astype(F32)
            second = (delta - first).astype(BF16).astype(F32)
            third = delta - first - second
            row = lax.broadcasted_iota(jnp.int32, (16, 128), 0)
            packed = jnp.where(row % 8 == 0, first, jnp.where(row % 8 == 1, second, third))
            out_ref[j, DEL0:MSG, :] = packed.astype(BF16)
    copies[2].wait()
    for pair in range(4):
        q = q_v[:, pl.ds(16 * pair, 16), :].astype(F32)
        for half in range(2):
            sub = slice(8 * half, 8 * half + 8)
            out_ref[2 * pair + half, 0:ROWS, :] = q[:, sub, :].reshape(ROWS, 128).astype(BF16)


def unpack_q_kernel(back_ref, q_hbm, q_v, sem):
    copies = []
    for pair in range(4):
        cols = pl.ds(16 * pair, 16)
        sides = [
            back_ref[2 * pair + half].astype(F32).reshape(TOK, 8, 128) for half in range(2)
        ]
        q_v[:, cols, :] = jnp.concatenate(sides, axis=1).astype(BF16)
        copies.append(
            pltpu.make_async_copy(q_v.at[:, cols, :], q_hbm.at[:, cols, :], sem.at[pair])
        )
        copies[-1].start()
    for copy in copies:
        copy.wait()


def unpack_kv_kernel(back_ref, k_hbm, v_hbm, k_v, v_v, wide, sem):
    copies = []
    for n, (src, dst) in enumerate(((k_v, k_hbm), (v_v, v_hbm))):
        for j in range(8):
            wide[n, pl.ds(j, TOK, 8), :] = back_ref[j, n * TOK : n * TOK + TOK, :].astype(F32)
        src[...] = wide[n].reshape(TOK, 8, 128).astype(BF16)
        copies.append(pltpu.make_async_copy(src, dst, sem.at[n]))
        copies[-1].start()
    for copy in copies:
        copy.wait()


def stored_block(core, c, i):
    y_hi = c % 2
    return linear(i // 2, core, c // 2, (i + c) % 2, y_hi)


def chunk_places(span_ref, core, c):
    first = core * 16 + c // 2 * 4 + c % 2
    even = first + c % 2 * 2
    odd = first + 2 - c % 2 * 2
    return [
        pl.multiple_of(span_ref[i // 2 * 32 + (odd if i % 2 else even)] * TOK, TOK)
        for i in range(8)
    ]


def attn_kernel(
    span_ref, start_ref, me_ref, msg_ref,
    kv0_ref, kv1_ref, mine0_ref, mine1_ref, mine2_ref, mine3_ref,
    theirs0_ref, theirs1_ref, theirs2_ref, theirs3_ref,
    dq_ref, part0_ref, part1_ref,
    unit_q, unit_at, k_s, kt_s, v_s, qt_s, gt_s, d_s, hi_s, lo_s, dk_s, dv_s, dq_s, m_s, l_s, w_s, s_s,
):
    core = me_ref[0]
    mine = me_ref[1]
    scale = 1.0 / math.sqrt(128)
    factor = scale * math.log2(math.e)

    k_s[LENGTH:, :] = jnp.zeros((PAD - LENGTH, 128), BF16)
    v_s[LENGTH:, :] = jnp.zeros((PAD - LENGTH, 128), BF16)

    share = [jnp.where(core == 0, a, b) for a, b in zip(*SHARE)]
    share_other = [jnp.where(core == 0, b, a) for a, b in zip(*SHARE)]
    chunks = [(kv0_ref, None, core, 0), (kv1_ref, None, 1 - core, 0)]
    chunks += [(mine3_ref, None, core, LAST), (theirs3_ref, None, 1 - core, LAST)]
    for n, ref in enumerate((mine0_ref, mine1_ref, mine2_ref)):
        chunks += [(ref, 0, core, share[n]), (ref, 1, 1 - core, share[n])]
    for n, ref in enumerate((theirs0_ref, theirs1_ref, theirs2_ref)):
        chunks += [(ref, 0, 1 - core, share_other[n]), (ref, 1, core, share_other[n])]
    for ref, side, who, e in chunks:
        for i, at in enumerate(chunk_places(span_ref, who, mine ^ e)):
            part = ref[i] if side is None else ref[side, i]
            k_s[pl.ds(at, TOK), :] = part[0:TOK]
            v_s[pl.ds(at, TOK), :] = part[TOK:PART]
    zero = jnp.zeros((256, 128), F32)
    for at in range(0, PAD, 256):
        dk_s[at : at + 256, :] = zero
        dv_s[at : at + 256, :] = zero
        kt_s[:, at : at + 256] = k_s[at : at + 256, :].T

    lane = lax.broadcasted_iota(jnp.int32, (8, ROWS), 1)
    sub = lax.broadcasted_iota(jnp.int32, (8, ROWS), 0)
    step = lax.broadcasted_iota(jnp.int32, (TK // 8, 8, ROWS), 0) * 8
    count = jnp.int32(0)
    for i in range(8):
        base = span_ref[stored_block(core, mine, i)] * TOK
        place_q = base + lane // GROUP
        begin = jnp.zeros((8, ROWS), jnp.int32)
        low = jnp.int32(0)
        for s in range(1, 8):
            edge = start_ref[s]
            begin = jnp.where(place_q >= edge, jnp.maximum(begin, edge), begin)
            low = jnp.where(base >= edge, jnp.maximum(low, edge), low)
        hi_s[i] = place_q - sub
        lo_s[i] = begin - sub
        first = low // 128 * 128
        tiles = (base + TOK - first + TK - 1) // TK

        def enlist(t, _):
            unit_q[count + t] = i
            unit_at[count + t] = first + t * TK
            return 0

        lax.fori_loop(0, tiles, enlist, 0)
        count = count + tiles
        qt_s[i] = msg_ref[i, 0:ROWS, :].T
        gt_s[i] = msg_ref[i, ROWS:DEL0, :].T
        tail = msg_ref[i, DEL0:MSG, :].astype(F32)
        halves = [tail[n : n + 1] + tail[n + 1 : n + 2] + tail[n + 2 : n + 3] for n in (0, 8)]
        d_s[i] = jnp.broadcast_to(jnp.concatenate(halves, axis=1), (8, ROWS))
        m_s[i] = jnp.full((8, ROWS), LOW, F32)
        l_s[i] = jnp.zeros((8, ROWS), F32)
        dq_s[i] = jnp.zeros((128, ROWS), F32)
    for n in range(WIDE - 1):
        unit_q[count + n] = 0
        unit_at[count + n] = LENGTH
    rounds = (count + WIDE - 1) // WIDE

    def units_of(n):
        units = []
        for u in range(WIDE):
            i = unit_q[n * WIDE + u]
            units.append((n % RING * WIDE + u, i, pl.multiple_of(unit_at[n * WIDE + u], 128)))
        return units

    def stats_dots(units):
        return [dot(k_s[pl.ds(at, TK), :], qt_s[i]) for _, i, at in units]

    def stats_rest(units, scores):
        results = []
        for (slot, i, at), s in zip(units, scores):
            s = (s * factor).reshape(TK // 8, 8, ROWS)
            upper = hi_s[i] - at
            span = (hi_s[i] - lo_s[i]).astype(jnp.uint32)
            back = (upper[None] - step).astype(jnp.uint32)
            s = jnp.where(back <= span[None], s, LOW)
            top = jnp.max(s, axis=0)
            e = jnp.exp2(s - top[None])
            s_s[slot] = e.reshape(TK, ROWS)
            w_s[slot] = top
            results.append((i, top, jnp.sum(e, axis=0)))
        for i, top, total in results:
            old = m_s[i]
            new = jnp.maximum(old, top)
            m_s[i] = new
            l_s[i] = l_s[i] * jnp.exp2(old - new) + total * jnp.exp2(top - new)

    def grads_dots(units):
        return [dot(v_s[pl.ds(at, TK), :], gt_s[i]) for _, i, at in units]

    def grads_soft(units, dps):
        results = []
        for (slot, i, at), dp in zip(units, dps):
            top = m_s[i]
            peak = jnp.max(top, axis=0, keepdims=True)
            total = jnp.sum(l_s[i] * jnp.exp2(top - peak), axis=0, keepdims=True)
            weight = jnp.exp2(w_s[slot] - peak) / total
            p = s_s[slot].reshape(TK // 8, 8, ROWS) * weight[None]
            ds = p * (dp.reshape(TK // 8, 8, ROWS) - d_s[i][None])
            p = p.reshape(TK, ROWS).astype(BF16)
            results.append((i, at, p, ds.reshape(TK, ROWS).astype(BF16)))
        return results

    def grads_rest(results):
        for i, at, p, ds in results:
            dv_s[pl.ds(at, TK), :] += dot(p, msg_ref[i, ROWS:DEL0, :])
            dk_s[pl.ds(at, TK), :] += dot(ds, msg_ref[i, 0:ROWS, :])
            dq_s[i] += dot(kt_s[:, pl.ds(at, TK)], ds)

    def ahead(n, _):
        for unit in units_of(n):
            stats_rest([unit], stats_dots([unit]))
        return 0

    def behind(n, _):
        units = units_of(n)
        grads_rest(grads_soft(units, grads_dots(units)))
        return 0

    def split(n, _):
        behind(n - LAG, 0)
        return ahead(n, 0)

    lax.fori_loop(0, jnp.minimum(rounds, LAG), ahead, 0)
    lax.fori_loop(LAG, rounds, split, 0)
    lax.fori_loop(jnp.maximum(rounds - LAG, 0), rounds, behind, 0)
    for i in range(8):
        dq_ref[i, :, :] = (dq_s[i] * scale).T.astype(BF16)

    for ref, me, flips in ((part0_ref, core, share), (part1_ref, 1 - core, share_other)):
        slots = [(who, e) for e in flips for who in (me, 1 - me)] + [(me, LAST), (me, 0)]
        for slot, (who, e) in enumerate(slots):
            for i, at in enumerate(chunk_places(span_ref, who, mine ^ e)):
                ref[slot, i, 0:TOK, :] = (dk_s[pl.ds(at, TOK), :] * scale).astype(BF16)
                ref[slot, i, TOK:PART, :] = dv_s[pl.ds(at, TOK), :].astype(BF16)


def vmem():
    return pl.BlockSpec(memory_space=pltpu.VMEM)


def smem():
    return pl.BlockSpec(memory_space=pltpu.SMEM)


def hbm():
    return pl.BlockSpec(memory_space=pl.ANY)


def cost(megabytes):
    return pl.CostEstimate(flops=0, bytes_accessed=megabytes << 20, transcendentals=0)


def pack_kv(keys, values):
    return pl.pallas_call(
        pack_kv_kernel,
        out_shape=jax.ShapeDtypeStruct((8, PART, 128), BF16),
        in_specs=[hbm()] * 2,
        out_specs=vmem(),
        scratch_shapes=[pltpu.VMEM((TOK, 8, 128), BF16)] * 2
        + [pltpu.VMEM((2, ROWS, 128), F32), pltpu.SemaphoreType.DMA((2,))],
        compiler_params=pltpu.CompilerParams(vmem_limit_bytes=58 << 20),
        name="pack_kv",
    )(keys, values)


def pack_q(queries, out_grads, out_states):
    return pl.pallas_call(
        pack_q_kernel,
        out_shape=jax.ShapeDtypeStruct((8, MSG, 128), BF16),
        in_specs=[hbm()] * 3,
        out_specs=vmem(),
        scratch_shapes=[pltpu.VMEM((TOK, 64, 128), BF16)] * 3 + [pltpu.SemaphoreType.DMA((3,))],
        compiler_params=pltpu.CompilerParams(vmem_limit_bytes=58 << 20),
        cost_estimate=cost(8),
        name="pack_q",
    )(queries, out_grads, out_states)


def unpack_q(back):
    return pl.pallas_call(
        unpack_q_kernel,
        out_shape=jax.ShapeDtypeStruct((TOK, 64, 128), BF16),
        in_specs=[vmem()],
        out_specs=hbm(),
        scratch_shapes=[pltpu.VMEM((TOK, 64, 128), BF16), pltpu.SemaphoreType.DMA((4,))],
        compiler_params=pltpu.CompilerParams(vmem_limit_bytes=58 << 20),
        cost_estimate=cost(6),
        name="unpack_q",
    )(back)


def unpack_kv(back):
    small = jax.ShapeDtypeStruct((TOK, 8, 128), BF16)
    return pl.pallas_call(
        unpack_kv_kernel,
        out_shape=(small, small),
        in_specs=[vmem()],
        out_specs=(hbm(),) * 2,
        scratch_shapes=[pltpu.VMEM((TOK, 8, 128), BF16)] * 2
        + [pltpu.VMEM((2, ROWS, 128), F32), pltpu.SemaphoreType.DMA((2,))],
        compiler_params=pltpu.CompilerParams(vmem_limit_bytes=58 << 20),
        name="unpack_kv",
    )(back)


def attention(span_position, starts, me, message, parts):
    kv_shape = jax.ShapeDtypeStruct((8, 8, PART, 128), BF16)
    return pl.pallas_call(
        attn_kernel,
        out_shape=(jax.ShapeDtypeStruct((8, ROWS, 128), BF16), kv_shape, kv_shape),
        in_specs=[smem()] * 3 + [vmem()] * 11,
        out_specs=(vmem(),) * 3,
        scratch_shapes=[
            pltpu.SMEM((UNITS,), jnp.int32),
            pltpu.SMEM((UNITS,), jnp.int32),
            pltpu.VMEM((PAD, 128), BF16),
            pltpu.VMEM((128, PAD), BF16),
            pltpu.VMEM((PAD, 128), BF16),
            pltpu.VMEM((8, 128, ROWS), BF16),
            pltpu.VMEM((8, 128, ROWS), BF16),
            pltpu.VMEM((8, 8, ROWS), F32),
            pltpu.VMEM((8, 8, ROWS), jnp.int32),
            pltpu.VMEM((8, 8, ROWS), jnp.int32),
            pltpu.VMEM((PAD, 128), F32),
            pltpu.VMEM((PAD, 128), F32),
            pltpu.VMEM((8, 128, ROWS), F32),
            pltpu.VMEM((8, 8, ROWS), F32),
            pltpu.VMEM((8, 8, ROWS), F32),
            pltpu.VMEM((RING * WIDE, 8, ROWS), F32),
            pltpu.VMEM((RING * WIDE, TK, ROWS), F32),
        ],
        compiler_params=pltpu.CompilerParams(vmem_limit_bytes=32 << 20),
        name="attention",
    )(span_position, starts, me, message, *parts)


def shards(queries, keys, values, out_states, out_grads, segment_ids, span_position):
    head = lax.axis_index("head")
    inner = lax.axis_index("inner")
    outer = lax.axis_index("outer")
    me = jnp.stack([head % 2, inner // 2 * 2 + outer]).astype(jnp.int32)
    starts = jnp.sum(
        segment_ids[None, :] < jnp.arange(8, dtype=jnp.int32)[:, None], axis=1, dtype=jnp.int32
    )
    kv = exchange(
        jnp.concatenate([keys.transpose(1, 0, 2), values.transpose(1, 0, 2)], axis=1)
    )
    message = pack_q(queries, out_grads, out_states)
    kv, message = lax.optimization_barrier((kv, message))
    kv_theirs = to_core(kv)
    kv_theirs, message = lax.optimization_barrier((kv_theirs, message))
    message = exchange(message)
    both = jnp.stack([kv, kv_theirs])
    got = [lax.ppermute(both, AXES, seq_pairs(flips)) for flips in zip(*SHARE)]
    got.append(lax.ppermute(kv, AXES, seq_pairs((LAST, LAST))))
    parts = [kv, kv_theirs] + got + [to_core(part) for part in got]
    dq, mine, other = attention(span_position, starts, me, message, parts)
    part = (mine.astype(F32) + to_core(other).astype(F32)).astype(BF16)
    dq = exchange(dq)
    got = [
        lax.ppermute(part[2 * n : 2 * n + 2], AXES, seq_pairs(flips)).astype(F32)
        for n, flips in enumerate(zip(*SHARE))
    ]
    last = lax.ppermute(part[6], AXES, seq_pairs((LAST, LAST)))
    total = part[7].astype(F32) + last.astype(F32) + got[0][0] + got[1][0] + got[2][0]
    give = got[0][1] + got[1][1] + got[2][1]
    total, give, dq = lax.optimization_barrier((total, give, dq))
    back = exchange((total + to_core(give)).astype(BF16))
    key_value = back.reshape(8, 2, TOK, 128).transpose(1, 2, 0, 3)
    return (
        unpack_q(dq),
        key_value[0],
        key_value[1],
    )


def solution(mesh):
    spec = P(AXES, None, None)
    return jax.shard_map(
        shards,
        mesh=mesh,
        in_specs=(spec,) * 5 + (P(), P()),
        out_specs=(spec,) * 3,
        check_vma=False,
    )
```
